128 devices in a mesh: cell: 16 (over y, x), sub: 8 (over z, core).
Axes of the slice: x: 4, y: 4, z: 4, core: 2. Of those that a mesh axis runs over, the one named last changes fastest.
Arguments:
- source: float32 [512, 384, 256], P('cell', 'sub'), may hold values from -60 to 60
- permeability: float32 [512, 384, 256], P('cell', 'sub'), may hold values from 0.2 to 5
- storage: float32 [512, 384, 256], P('cell', 'sub'), may hold values from 1 to 10
- face_cell: int32 [262144], P(('cell', 'sub')), may hold values from 0 to 393215
- face_dest: int32 [262144, 1], P(('cell', 'sub')), may hold values from 0 to 127; in each aligned block of 2048 rows (0 to 2047, 2048 to 4095, ...) at most 32 rows name the same one
- face_dof: int32 [262144], P(('cell', 'sub')), may hold values from 0 to 3071
- face_weight: float32 [262144], P(('cell', 'sub')), may hold values from -6 to 6
- tectonic_load: float32 [512, 768], P(('cell', 'sub')), may hold values from -6 to 6
- patch_matrix: float32 [512, 768, 768], P(('cell', 'sub')), as said below
- yield_limit: float32 [512, 768], P(('cell', 'sub')), may hold values from 0.2 to 2
- free_mask: int32 [4, 512, 768], P(None, ('cell', 'sub')), may hold values 0 or 1
- step_kind: int32 [4, 512], P(None, ('cell', 'sub')), may hold values from 0 to 2
Outputs:
- pressure_change: float32 [512, 384, 256], P('cell', 'sub')
- slip: float32 [512, 768], P(('cell', 'sub'))
The draws below stay inside these ranges and needn't reach their ends.
Inputs may be any that keep to these rules, and one draw needn't show every extreme that they name: `face_dest`: within the faces of one block (aligned blocks of 2048 rows) no owner is named more than 32 times, and in every draw some block names some owner exactly 32 times. `face_cell`: flattened index of the cell inside the block that holds the face. `face_dof`: index patch-major over the owner's 4 patches. `free_mask`: 1 marks a free unknown. `step_kind`: 0: conjugate step on the free unknowns, 1: proportioning step along the chopped gradient, 2: expansion step along the full gradient. `patch_matrix`: each patch's matrix is symmetric positive definite.
All inputs are finite; a program needn't handle non-finite values. No bound on the sum of `free_mask` on one device may be relied on, other than what follows from the above.
Results may differ from the reference program's by a relative error of at most 0.00011.
Values sent between devices are 32-bit elements; how exact they have to be, the bound alone decides.
No kernel may reach another device: no remote copies, remote signals or barrier semaphores. Data moves between devices by JAX's collectives and lax.ppermute only.
A program may use at most 128 MiB of HBM per device.

```python
import math
import jax
import jax.numpy as jnp
import numpy as np
from jax import lax

CX = 32
CY = 48
CZ = 256
FACE_DEV = 2048
DOF = 768
PATCH_DEV = 4
PRES_ITERS = 2
FRIC_ITERS = 4
NX = 512
NY = 384
FACES = 262144
PATCHES = 512
CAP = 32
N_CELL = 16
N_SUB = 8
DEVICES = 128


def draw_patch_matrix(key, part):
    key = jax.random.fold_in(key, 11)
    key_entry = jax.random.fold_in(key, 1)
    key_lift = jax.random.fold_in(key, 2)
    key_across = jax.random.fold_in(key, 4)
    key_along = jax.random.fold_in(key, 5)
    reach = 1.5
    amplitude = 0.3
    side_long = jnp.sqrt(jnp.float32(DOF) * 4.0 / 3.0)
    side_short = jnp.float32(DOF) / side_long
    node_across = jax.random.uniform(key_across, (PATCHES, DOF), jnp.float32, 0.0, 1.0) * side_long
    node_along = jax.random.uniform(key_along, (PATCHES, DOF), jnp.float32, 0.0, 1.0) * side_short
    gap_across = node_across[:, :, None] - node_across[:, None, :]
    gap_along = node_along[:, :, None] - node_along[:, None, :]
    distance = jnp.sqrt(gap_across * gap_across + gap_along * gap_along)
    kernel = jnp.exp(-distance / reach)
    raw_uniform = jax.random.uniform(key_entry, (PATCHES, DOF, DOF), jnp.float32, -1.0, 1.0)
    identity = jnp.eye(DOF, dtype=jnp.float32)
    scattered = 0.5 * (raw_uniform + jnp.swapaxes(raw_uniform, 1, 2)) * (1.0 - identity) * (0.5 / DOF)
    diag_lift = jax.random.uniform(key_lift, (PATCHES, DOF), jnp.float32, 1.2, 2.0)
    matrix = (scattered + identity * diag_lift[:, :, None] + amplitude * kernel) / 1.5
    return matrix


def plant(entries, own_key, least, top_value):
    spot = [jax.random.randint(jax.random.fold_in(own_key, axis), (), 0, length) for axis, length in enumerate(entries.shape)]
    longest = entries.shape.index(max(entries.shape))
    next_to = spot[:longest] + [(spot[longest] + 1) % entries.shape[longest]] + spot[longest + 1:]
    return entries.at[tuple(spot)].set(least).at[tuple(next_to)].set(top_value)


def level_of(own_key, shape, cuts, low, high):
    def one(dim, parts):
        heights = jax.random.uniform(jax.random.fold_in(jax.random.fold_in(own_key, 6), dim), (parts,), jnp.float32, low / len(cuts), high / len(cuts))
        return jnp.repeat(jnp.exp(heights), shape[dim] // parts).reshape((-1,) + (1,) * (len(shape) - dim - 1))

    factor_of = one(*cuts[0])
    for cut in cuts[1:]:
        factor_of = factor_of * one(*cut)
    return factor_of


def routed_block(key, own, number, rows, number_of, top, bound, slope):
    ranking = jax.random.permutation(key, number_of)
    packed, common = load_shares(number_of, rows * top, bound, slope, True), load_shares(number_of, rows * top, bound, slope, False)
    places = jnp.arange(number_of)

    def named(tallies, rotation):
        used = int((tallies > 0).sum())
        fixed = max(1, used // 4)
        shifted = fixed + (places - fixed + rotation * (used - fixed)) % max(1, number_of - fixed)
        return jnp.zeros((number_of,), jnp.int32).at[ranking[jnp.where(places < fixed, places, shifted)]].set(jnp.asarray(tallies, jnp.int32))

    tallies = jnp.where(number % 4 == 0, named(packed, number // 4), named(common, number - number // 4 - 1))
    mixed = jax.random.permutation(jax.random.fold_in(own, 3), number_of)
    giver, taker = mixed[0:number_of // 2 * 2:2], mixed[1:number_of // 2 * 2:2]
    margin = jnp.minimum(tallies[giver] - 1, bound - tallies[taker]) // 2
    margin = jnp.where((giver == ranking[0]) | (taker == ranking[0]) | (tallies[taker] == 0), 0, jnp.maximum(margin, 0))
    shifted = jax.random.randint(jax.random.fold_in(own, 4), (number_of // 2,), 0, 1 << 20) % (margin + 1)
    tallies = tallies.at[giver].add(-shifted).at[taker].add(shifted)
    labels = jnp.searchsorted(jnp.cumsum(tallies), jnp.arange(rows * top), side="right").astype(jnp.int32)
    table = labels.reshape(top, rows).T
    table = table[jax.random.permutation(jax.random.fold_in(own, 1), rows)]
    rotation = jax.random.randint(jax.random.fold_in(own, 2), (rows, 1), 0, top)
    return jnp.take_along_axis(table, (jnp.arange(top)[None, :] + rotation) % top, axis=1)


def load_shares(count, total, most, lean, full):
    loads = [(1 << 20) // math.isqrt(rank ** lean) + 1 for rank in range(1, count + 1)]
    largest = most if full else min(most, max(-(-total // count), total * loads[0] // sum(loads)))
    least = 1 if total - largest >= count - 1 else 0
    given, surplus = [largest] + [least] * (count - 1), total - largest - least * (count - 1)
    while surplus > 0:
        movable = [i for i in range(1, count) if given[i] < largest] or [i for i in range(1, count) if given[i] < most]
        pool, left = sum([loads[i] for i in movable]), surplus
        for i in movable:
            addition = min(most - given[i], max(1, left * loads[i] // pool), surplus)
            given[i] = given[i] + addition
            surplus = surplus - addition
    return np.array(given)


def bell_draw(rng, extent, scale, most, shards=(), kind=jnp.bfloat16):
    result = scale * jax.random.normal(rng, extent, jnp.float32)
    if shards:
        result = result * level_of(rng, extent, shards, -0.22, 0.18)
    return jnp.clip(result, -most, most).astype(kind)


def setup_inputs(seed: int = 0) -> dict:
    arg_keys = jax.random.split(jax.random.key(seed), 13)
    source = bell_draw(arg_keys[0], (NX, NY, CZ), 10.0, 60.0, ((0, 16), (1, 8)), jnp.float32)
    permeability = jnp.clip(jnp.exp(math.log(5.0) - 3.218876 * jax.random.uniform(arg_keys[1], (NX, NY, CZ), jnp.float32) ** level_of(arg_keys[1], (NX, NY, CZ), ((0, 16), (1, 8)), -0.2, 0.2)), 0.2, 5.0)
    storage = jnp.clip(jnp.exp(math.log(10.0) - 2.3025851 * jax.random.uniform(arg_keys[2], (NX, NY, CZ), jnp.float32) ** level_of(arg_keys[2], (NX, NY, CZ), ((0, 16), (1, 8)), -0.2, 0.2)), 1.0, 10.0)
    face_cell = plant(jax.random.randint(arg_keys[3], (FACES,), 0, CX * CY * CZ), jax.random.fold_in(arg_keys[3], 1), 0, (CX * CY * CZ) - 1).astype(jnp.int32)
    face_dest_keys = jax.random.split(jax.random.fold_in(arg_keys[4], 1), FACES // FACE_DEV)
    face_dest_turns = jax.random.permutation(jax.random.fold_in(arg_keys[4], 3), FACES // FACE_DEV)
    face_dest = jax.vmap(lambda own, number: routed_block(jax.random.fold_in(arg_keys[4], 2), own, number, FACE_DEV, DEVICES, 1, CAP, 2))(face_dest_keys, face_dest_turns).reshape((FACES, 1))
    face_dof = plant(jax.random.randint(arg_keys[5], (FACES,), 0, PATCH_DEV * DOF), jax.random.fold_in(arg_keys[5], 1), 0, (PATCH_DEV * DOF) - 1).astype(jnp.int32)
    face_weight = bell_draw(arg_keys[6], (FACES,), 1.0, 6.0, ((0, 128),), jnp.float32)
    tectonic_load = bell_draw(arg_keys[7], (PATCHES, DOF), 1.0, 6.0, ((0, 128),), jnp.float32)
    patch_matrix = draw_patch_matrix(jax.random.fold_in(arg_keys[12], 71), 0)
    yield_limit = jnp.clip(jnp.exp(math.log(2.0) - 2.3025851 * jax.random.uniform(arg_keys[9], (PATCHES, DOF), jnp.float32) ** level_of(arg_keys[9], (PATCHES, DOF), ((0, 128),), -0.2, 0.2)), 0.2, 2.0)
    free_mask = plant((jax.random.randint(arg_keys[10], (FRIC_ITERS, PATCHES, DOF), 0, 4) < 3).astype(jnp.int32), jax.random.fold_in(arg_keys[10], 1), 0, 1)
    step_kind = plant(jax.random.randint(arg_keys[11], (FRIC_ITERS, PATCHES), 0, 3), jax.random.fold_in(arg_keys[11], 1), 0, 2).astype(jnp.int32)
    return {"source": source, "permeability": permeability, "storage": storage, "face_cell": face_cell, "face_dest": face_dest, "face_dof": face_dof, "face_weight": face_weight, "tectonic_load": tectonic_load, "patch_matrix": patch_matrix, "yield_limit": yield_limit, "free_mask": free_mask, "step_kind": step_kind}


HIGHEST = lax.Precision.HIGHEST


def harmonic(here_perm, there_perm):
    return 2.0 * here_perm * there_perm / (here_perm + there_perm)


def neighbours(padded):
    return (padded[2:, 1:-1, 1:-1], padded[:-2, 1:-1, 1:-1],
            padded[1:-1, 2:, 1:-1], padded[1:-1, :-2, 1:-1],
            padded[1:-1, 1:-1, 2:], padded[1:-1, 1:-1, :-2])


def apply_flow(field_in, permeability, storage):
    perm_sides = neighbours(jnp.pad(permeability, 1))
    field_sides = neighbours(jnp.pad(field_in, 1))
    summed = storage * field_in
    for perm_side, near_value in zip(perm_sides, field_sides):
        summed = summed + harmonic(permeability, perm_side) * (field_in - near_value)
    return summed


def patch_solve(patch_matrix, fault_load, yield_limit, free_mask, step_kind):
    slip_now = jnp.zeros_like(fault_load)
    previous = jnp.zeros_like(fault_load)
    previous_image = jnp.zeros_like(fault_load)
    for iteration in range(FRIC_ITERS):
        gradient = jnp.einsum("pij,pj->pi", patch_matrix, slip_now, precision=HIGHEST) - fault_load
        free_now = free_mask[iteration].astype(jnp.float32)
        kind_now = step_kind[iteration][:, None]
        free_part = free_now * gradient
        chopped = (1.0 - free_now) * gradient
        conjugacy = jnp.mean(free_part * previous_image, axis=1, keepdims=True) / (
            jnp.mean(previous * previous_image, axis=1, keepdims=True) + 1e-6)
        direction = jnp.where(kind_now == 0, free_part - conjugacy * previous,
                              jnp.where(kind_now == 1, chopped, gradient))
        image_vec = jnp.einsum("pij,pj->pi", patch_matrix, direction, precision=HIGHEST)
        step_length = jnp.mean(gradient * direction, axis=1, keepdims=True) / (
            jnp.mean(direction * image_vec, axis=1, keepdims=True) + 1e-6)
        slip_now = jnp.clip(slip_now - step_length * direction, -yield_limit, yield_limit)
        previous = direction
        previous_image = image_vec
    return slip_now


def reference(source, permeability, storage, face_cell, face_dest, face_dof, face_weight,
              tectonic_load, patch_matrix, yield_limit, free_mask, step_kind):
    pressure_change = jnp.zeros_like(source)
    residual = source
    direction = source
    norm_now = jnp.sum(residual * residual)
    for iteration in range(PRES_ITERS):
        image_field = apply_flow(direction, permeability, storage)
        step_length = norm_now / jnp.sum(direction * image_field)
        pressure_change = pressure_change + step_length * direction
        residual = residual - step_length * image_field
        norm_next = jnp.sum(residual * residual)
        direction = residual + (norm_next / norm_now) * direction
        norm_now = norm_next
    block_cells = CX * CY * CZ
    flattened = pressure_change.reshape(N_CELL, CX, N_SUB, CY, CZ).transpose(0, 2, 1, 3, 4).reshape(-1)
    block_of_face = jnp.arange(FACES, dtype=jnp.int32) // FACE_DEV
    face_values = face_weight * flattened[block_of_face * block_cells + face_cell]
    segment_ids = face_dest[:, 0] * (PATCH_DEV * DOF) + face_dof
    fault_load = tectonic_load.reshape(-1) + jax.ops.segment_sum(face_values, segment_ids, num_segments=PATCHES * DOF)
    fault_load = fault_load.reshape(PATCHES, DOF)
    slip = patch_solve(patch_matrix, fault_load, yield_limit, free_mask, step_kind)
    return pressure_change, slip
```

```python
import jax
import jax.numpy as jnp
from jax import lax
from jax.sharding import PartitionSpec as P

FRIC_ITERS = 4
SLOTS = 32
HIGHEST = lax.Precision.HIGHEST
AXES = ("cell", "sub")


def swap_halo(head, tail, axis):
    count = lax.axis_size(axis)
    even = lax.axis_index(axis) % 2 == 0
    first = [(i, i ^ 1) for i in range(count)]
    second = [(i, i + 1) for i in range(1, count - 1, 2)]
    second = second + [(j, i) for i, j in second]
    got_first = lax.ppermute(jnp.where(even, tail, head), axis, first)
    got_second = lax.ppermute(jnp.where(even, head, tail), axis, second)
    return jnp.where(even, got_second, got_first), jnp.where(even, got_first, got_second)


def harmonic(here_perm, there_perm):
    return 2.0 * here_perm * there_perm / (here_perm + there_perm)


def extend(fields):
    lo, hi = swap_halo(fields[:, 0], fields[:, -1], "cell")
    low, high = swap_halo(fields[:, :, 0], fields[:, :, -1], "sub")
    inner = jnp.concatenate([lo[:, None], fields, hi[:, None]], axis=1)
    grow = lambda side: jnp.pad(side, ((0, 0), (1, 1), (0, 0)))[:, :, None]
    inner = jnp.concatenate([grow(low), inner, grow(high)], axis=2)
    return jnp.pad(inner, ((0, 0), (0, 0), (0, 0), (1, 1)))


def after(padded):
    return padded[2:, 1:-1, 1:-1], padded[1:-1, 2:, 1:-1], padded[1:-1, 1:-1, 2:]


def before(padded):
    return padded[:-2, 1:-1, 1:-1], padded[1:-1, :-2, 1:-1], padded[1:-1, 1:-1, :-2]


def slot_maps(face_dest, owners):
    faces = face_dest.shape[0]
    chunk = 128
    named = (face_dest == jnp.arange(owners)[None, :]).astype(jnp.bfloat16)
    blocks = named.reshape(faces // chunk, chunk, owners)
    lower = jnp.tril(jnp.ones((chunk, chunk), jnp.bfloat16), -1)
    within = jnp.einsum("ij,cjo->cio", lower, blocks, preferred_element_type=jnp.float32)
    totals = jnp.sum(blocks.astype(jnp.float32), axis=1)
    start = jnp.cumsum(totals, axis=0) - totals
    rank = jnp.sum((within + start[:, None]) * blocks.astype(jnp.float32), axis=2).reshape(faces)
    slot = (rank[:, None] == jnp.arange(SLOTS, dtype=jnp.float32)[None, :]).astype(jnp.float32)
    return named.astype(jnp.float32), slot


def patch_solve(patch_matrix, fault_load, yield_limit, free_mask, step_kind):
    slip_now = jnp.zeros_like(fault_load)
    previous = jnp.zeros_like(fault_load)
    previous_image = jnp.zeros_like(fault_load)
    for iteration in range(FRIC_ITERS):
        if iteration == 0:
            gradient = -fault_load
        else:
            gradient = jnp.einsum("pij,pj->pi", patch_matrix, slip_now, precision=HIGHEST) - fault_load
        free_now = free_mask[iteration].astype(jnp.float32)
        kind_now = step_kind[iteration][:, None]
        free_part = free_now * gradient
        chopped = (1.0 - free_now) * gradient
        conjugacy = jnp.mean(free_part * previous_image, axis=1, keepdims=True) / (
            jnp.mean(previous * previous_image, axis=1, keepdims=True) + 1e-06
        )
        direction = jnp.where(
            kind_now == 0,
            free_part - conjugacy * previous,
            jnp.where(kind_now == 1, chopped, gradient),
        )
        image_vec = jnp.einsum("pij,pj->pi", patch_matrix, direction, precision=HIGHEST)
        step_length = jnp.mean(gradient * direction, axis=1, keepdims=True) / (
            jnp.mean(direction * image_vec, axis=1, keepdims=True) + 1e-06
        )
        slip_now = jnp.clip(slip_now - step_length * direction, -yield_limit, yield_limit)
        previous = direction
        previous_image = image_vec
    return slip_now


def on_device(
    source,
    permeability,
    storage,
    face_cell,
    face_dest,
    face_dof,
    face_weight,
    tectonic_load,
    patch_matrix,
    yield_limit,
    free_mask,
    step_kind,
):
    devices = lax.axis_size(AXES)
    both = extend(jnp.stack([source, permeability]))
    source_ext, perm_ext = both[0], both[1]
    conduct_after = [harmonic(permeability, side) for side in after(perm_ext)]
    conduct_before = [harmonic(permeability, side) for side in before(perm_ext)]
    image = storage * source
    for conduct, near in zip(conduct_after + conduct_before, after(source_ext) + before(source_ext)):
        image = image + conduct * (source - near)

    square = jnp.sum(source * source)
    mu = jnp.where(square > 0.0, jnp.sum(source * image) / jnp.where(square > 0.0, square, 1.0), 0.0)
    image_ext = extend(image[None])[0]
    rest_ext = image_ext - mu * source_ext
    rest = image - mu * source
    bb = jnp.sum(storage * source * source)
    bv = jnp.sum(storage * source * rest)
    vv = jnp.sum(storage * rest * rest)
    for conduct, b_near, v_near in zip(conduct_after, after(source_ext), after(rest_ext)):
        db, dv = source - b_near, rest - v_near
        bb = bb + jnp.sum(conduct * db * db)
        bv = bv + jnp.sum(conduct * db * dv)
        vv = vv + jnp.sum(conduct * dv * dv)
    scalars = jnp.stack([square, mu, jnp.sum(rest * rest), bb, bv, vv, bb, vv])

    named, slot = slot_maps(face_dest, devices)
    values = [
        face_dof.astype(jnp.float32),
        face_weight * source.reshape(-1)[face_cell],
        face_weight * image.reshape(-1)[face_cell],
    ]
    spread = jnp.concatenate([slot * value[:, None] for value in values], axis=1)
    sent = jnp.einsum("fo,fs->os", named, spread, precision=HIGHEST)
    sent = jnp.concatenate([sent, jnp.broadcast_to(scalars[None], (devices, 8)), jnp.zeros((devices, 24))], axis=1)
    got = lax.all_to_all(sent, AXES, 0, 0, tiled=True)

    scal = got[:, 3 * SLOTS : 3 * SLOTS + 6]
    square, mu, rest_sq, bb, bv, vv = [scal[:, i] for i in range(6)]
    norm = jnp.sum(square)
    alpha = norm / jnp.sum(bb)
    part = 1.0 - alpha * mu
    norm_next = jnp.sum((part * jnp.sqrt(square)) ** 2 + alpha * alpha * rest_sq)
    beta = norm_next / norm
    part = part + beta
    curve = jnp.sum(part * part * bb - 2.0 * part * alpha * bv + alpha * alpha * vv)
    alpha_next = norm_next / curve
    on_source = alpha + alpha_next * (1.0 + beta)
    on_image = -alpha_next * alpha
    pressure_change = on_source * source + on_image * image

    width = tectonic_load.shape[0] * tectonic_load.shape[1]
    dof = got[:, :SLOTS].reshape(-1).astype(jnp.int32)
    load_terms = (on_source * got[:, SLOTS : 2 * SLOTS] + on_image * got[:, 2 * SLOTS : 3 * SLOTS]).reshape(-1)
    tall = (dof[None] // 128 == jnp.arange(width // 128)[:, None]).astype(jnp.float32) * load_terms[None]
    wide = (dof[None] % 128 == jnp.arange(128)[:, None]).astype(jnp.float32)
    loads = jnp.einsum("he,le->hl", tall, wide, precision=HIGHEST)
    fault_load = tectonic_load + loads.reshape(tectonic_load.shape)
    slip = patch_solve(patch_matrix, fault_load, yield_limit, free_mask, step_kind)
    return (pressure_change, slip)


def solution(mesh):
    return jax.shard_map(
        on_device,
        mesh=mesh,
        in_specs=(
            P("cell", "sub", None),
            P("cell", "sub", None),
            P("cell", "sub", None),
            P(("cell", "sub")),
            P(("cell", "sub"), None),
            P(("cell", "sub")),
            P(("cell", "sub")),
            P(("cell", "sub"), None),
            P(("cell", "sub"), None, None),
            P(("cell", "sub"), None),
            P(None, ("cell", "sub"), None),
            P(None, ("cell", "sub")),
        ),
        out_specs=(P("cell", "sub", None), P(("cell", "sub"), None)),
        check_vma=False,
    )
```

```python
import functools

import jax
import jax.numpy as jnp
from jax import lax
from jax.experimental import pallas as pl
from jax.experimental.pallas import tpu as pltpu
from jax.sharding import PartitionSpec as P

SLOTS = 32
AXES = ("cell", "sub")
LANES = 128


def split3(values):
    first = values.astype(jnp.bfloat16).astype(jnp.float32)
    left = values - first
    second = left.astype(jnp.bfloat16).astype(jnp.float32)
    return first, second, left - second


def to_columns(block):
    return block.T


def onehot(values):
    return values.astype(jnp.float32).astype(jnp.bfloat16)


def pick_lane(gathered, lane_column):
    lane = lax.broadcasted_iota(jnp.int32, gathered.shape, 1).astype(jnp.float32)
    return jnp.sum(jnp.where(lane == lane_column, gathered, 0.0), axis=1, keepdims=True)


def grouped_pieces(value, rank):
    lane = lax.broadcasted_iota(jnp.int32, (value.shape[0], LANES), 1)
    first, second, third = split3(value)
    piece = jnp.where(lane < SLOTS, first, jnp.where(lane < 2 * SLOTS, second, third))
    here = ((lane & (SLOTS - 1)).astype(jnp.float32) == rank) & (lane < 3 * SLOTS)
    return jnp.where(here, piece, 0.0).astype(jnp.bfloat16)


def join_groups(summed, group):
    lane = lax.broadcasted_iota(jnp.int32, summed.shape, 1)
    joined = summed + pltpu.roll(summed, LANES - SLOTS, 1) + pltpu.roll(summed, LANES - 2 * SLOTS, 1)
    if group:
        joined = pltpu.roll(joined, group * SLOTS, 1)
    return jnp.where((lane >= group * SLOTS) & (lane < (group + 1) * SLOTS), joined, 0.0)


def copy_rows(table, picks, where_ref, first, count):
    for j in range(count):
        picks[pl.ds(first + j, 1), :] = table[pl.ds(where_ref[first + j], 1), :]


def faces_kernel(
    where_ref,
    dest_ref,
    code_ref,
    weight_ref,
    lane_ref,
    source_ref,
    sent_ref,
    columns_ref,
    table,
    picks,
    owners,
    spread,
    sems,
):
    chunks = dest_ref.shape[0]
    rows = source_ref.shape[0]
    halves = [
        pltpu.make_async_copy(
            source_ref.at[:, pl.ds(t * LANES, LANES)], table.at[pl.ds(t * rows, rows), :], sems.at[t]
        )
        for t in range(2)
    ]
    for half in halves:
        half.start()
    dest = dest_ref[...].astype(jnp.float32)
    dest_columns = to_columns(dest)
    code_columns = to_columns(code_ref[...])
    weight_columns = to_columns(weight_ref[...])
    lane_columns = to_columns(lane_ref[...].astype(jnp.float32))
    lane = lax.broadcasted_iota(jnp.int32, (LANES, LANES), 1)
    row = lax.broadcasted_iota(jnp.int32, (LANES, LANES), 0)
    lower = onehot(lane < row)
    lane_number = lane.astype(jnp.float32)
    start = jnp.zeros((1, LANES), jnp.float32)
    ranks = []
    for c in range(chunks):
        named = (lane_number == dest_columns[:, c : c + 1]).astype(jnp.float32)
        ahead = jnp.dot(lower, named.astype(jnp.bfloat16), preferred_element_type=jnp.float32)
        ranks.append(jnp.sum(named * (ahead + start), axis=1, keepdims=True))
        start = start + jnp.sum(named, axis=0, keepdims=True)
    columns_ref[...] = jnp.zeros_like(columns_ref)
    for c in range(chunks):
        columns_ref[:, c : c + 1] = ranks[c]
    columns_ref[:, chunks : 2 * chunks] = weight_columns
    columns_ref[:, 2 * chunks : 3 * chunks] = lane_columns
    for half in halves:
        half.wait()

    def gather(i, carry):
        copy_rows(table, picks, where_ref, i * 64, 64)
        return carry

    lax.fori_loop(0, chunks * LANES // 64, gather, 0)
    row_number = row.astype(jnp.float32)
    for c in range(chunks):
        span = pl.ds(c * LANES, LANES)
        owners[:, span] = onehot(row_number == dest[c : c + 1, :])
        value = weight_columns[:, c : c + 1] * pick_lane(picks[span, :], lane_columns[:, c : c + 1])
        spread[span, :LANES] = grouped_pieces(code_columns[:, c : c + 1], ranks[c])
        spread[span, LANES:] = grouped_pieces(value, ranks[c])
    summed = jnp.dot(owners[...], spread[...], preferred_element_type=jnp.float32)
    sent_ref[...] = join_groups(summed[:, :LANES], 0) + join_groups(summed[:, LANES:], 1)


def faces(source, where, lane, dest, code, weight):
    count = where.shape[0]
    chunks = count // LANES
    rows = source.shape[0] * source.shape[1]
    vmem = pl.BlockSpec(memory_space=pltpu.VMEM)
    cut = lambda values: values.reshape(chunks, LANES)
    return pl.pallas_call(
        faces_kernel,
        out_shape=(
            jax.ShapeDtypeStruct((LANES, LANES), jnp.float32),
            jax.ShapeDtypeStruct((LANES, LANES), jnp.float32),
        ),
        in_specs=[pl.BlockSpec(memory_space=pltpu.SMEM)] + [vmem] * 4 + [pl.BlockSpec(memory_space=pl.ANY)],
        out_specs=(vmem, vmem),
        scratch_shapes=[
            pltpu.VMEM((2 * rows, LANES), jnp.float32),
            pltpu.VMEM((count, LANES), jnp.float32),
            pltpu.VMEM((LANES, count), jnp.bfloat16),
            pltpu.VMEM((count, 2 * LANES), jnp.bfloat16),
            pltpu.SemaphoreType.DMA((2,)),
        ],
        compiler_params=pltpu.CompilerParams(vmem_limit_bytes=12 * 2**20),
        name="faces",
    )(where, cut(dest), cut(code), cut(weight), cut(lane), source.reshape(rows, source.shape[2]))


def image_kernel(
    where_ref,
    even_ref,
    dest_ref,
    columns_ref,
    sent_in_ref,
    cell_first_ref,
    cell_second_ref,
    sub_first_ref,
    sub_second_ref,
    source_ref,
    perm_ref,
    storage_ref,
    image_ref,
    sent_ref,
    field,
    half,
    store,
    image,
    flow_x,
    flow_y,
    flow_z,
    con_x,
    con_y,
    con_z,
    carry_x,
    table,
    picks,
    owners,
    spread,
    sems,
):
    planes, height, depth = source_ref.shape
    strips = height // 8
    group = 8
    copies = []
    for g in range(planes // group):
        for n, (array, held, shift) in enumerate(
            ((source_ref, field, 1), (perm_ref, half, 1), (storage_ref, store, 0))
        ):
            copies.append(
                pltpu.make_async_copy(
                    array.at[pl.ds(g * group, group)],
                    held.at[pl.ds(shift + g * group, group), pl.ds(8, height), :],
                    sems.at[3 * g + n],
                )
            )
    for copy in copies:
        copy.start()

    even_cell = even_ref[0] == 1
    even_sub = even_ref[1] == 1
    own = pl.ds(8, height)

    def cell_side(n):
        one, two = cell_first_ref[n], cell_second_ref[n]
        return jnp.where(even_cell, two, one), jnp.where(even_cell, one, two)

    lo, hi = cell_side(0)
    field[0, own, :] = lo
    field[planes + 1, own, :] = hi
    field[planes + 2, own, :] = cell_side(1)[1]
    lo, hi = cell_side(2)
    half[0, own, :] = lo
    half[planes + 1, own, :] = hi
    half[planes + 2, own, :] = cell_side(3)[1]
    store[planes, own, :] = cell_side(4)[1]

    def sub_side(n):
        one, two = sub_first_ref[n], sub_second_ref[n]
        return jnp.where(even_sub, two, one), jnp.where(even_sub, one, two)

    edge = 8 + height
    b_lo, b_hi = sub_side(0)
    b_far = sub_side(1)[1]
    k_lo, k_hi = sub_side(2)
    k_far = sub_side(3)[1]
    s_hi = sub_side(4)[1]
    for x in range(planes + 2):
        field[x, 7:8, :] = b_lo[x : x + 1]
        field[x, edge : edge + 1, :] = b_hi[x : x + 1]
        field[x, edge + 1 : edge + 2, :] = b_far[x : x + 1]
        half[x, 7:8, :] = k_lo[x : x + 1]
        half[x, edge : edge + 1, :] = k_hi[x : x + 1]
        half[x, edge + 1 : edge + 2, :] = k_far[x : x + 1]
        if x >= 1:
            store[x - 1, edge : edge + 1, :] = s_hi[x : x + 1]

    lane = lax.broadcasted_iota(jnp.int32, (8, depth), 1)
    row = lax.broadcasted_iota(jnp.int32, (8, depth), 0)

    def halve(x):
        half[x] = 0.5 / jnp.maximum(half[x], 1e-30)

    def first_x():
        for i in range(strips + 1):
            rows = pl.ds(8 + 8 * i, 8)
            conduct = 1.0 / (half[0, rows, :] + half[1, rows, :])
            carry_x[rows, :] = conduct * (field[0, rows, :] - field[1, rows, :])

    def plane(x, sums, inside):
        halve(x + 2)
        sums = list(sums)
        here_b, here_h = field[x + 1, 0:8, :], half[x + 1, 0:8, :]
        last_y = (here_b - field[x + 1, 1:9, :]) / (here_h + half[x + 1, 1:9, :])
        for i in range(strips + 1):
            at = 8 + 8 * i
            rows = pl.ds(at, 8)
            b, h, s = field[x + 1, rows, :], half[x + 1, rows, :], store[x, rows, :]
            if i < strips:
                b_y, h_y = field[x + 1, pl.ds(at + 1, 8), :], half[x + 1, pl.ds(at + 1, 8), :]
            else:
                b_y, h_y = pltpu.roll(b, 7, 0), pltpu.roll(h, 7, 0)
            b_x, h_x = field[x + 2, rows, :], half[x + 2, rows, :]
            c_x = 1.0 / (h + h_x)
            c_y = 1.0 / (h + h_y)
            c_z = jnp.where(lane == depth - 1, 0.0, 1.0 / (h + pltpu.roll(h, depth - 1, 1)))
            d_x, d_y, d_z = b - b_x, b - b_y, b - pltpu.roll(b, depth - 1, 1)
            f_x, f_y, f_z = c_x * d_x, c_y * d_y, c_z * d_z
            came_y = pltpu.roll(jnp.where(row == 7, last_y, f_y), 1, 0)
            sb = s * b
            w = sb + (f_x - carry_x[rows, :]) + (f_y - came_y) + (f_z - pltpu.roll(f_z, 1, 1))
            carry_x[rows, :] = f_x
            last_y = f_y
            image[x, rows, :] = w
            if inside and i < strips:
                out = pl.ds(8 * i, 8)
                image_ref[x, out, :] = w
                for t in range(2):
                    table[pl.ds(pl.multiple_of((t * planes + x) * height, 8) + 8 * i, 8), :] = w[
                        :, t * LANES : (t + 1) * LANES
                    ]
                con_x[x, out, :] = c_x
                con_y[x, out, :] = c_y
                con_z[x, out, :] = c_z
                flow_x[x, out, :] = f_x
                flow_y[x, out, :] = f_y
                flow_z[x, out, :] = f_z
                sums[0] = sums[0] + b * b
                sums[1] = sums[1] + b * w
                sums[2] = sums[2] + (sb * b + f_x * d_x) + (f_y * d_y + f_z * d_z)
        return tuple(sums)

    zero = jnp.zeros((8, depth), jnp.float32)
    sums = (zero, zero, zero)
    for g in range(planes // group):
        for copy in copies[3 * g : 3 * g + 3]:
            copy.wait()
        if g == 0:
            halve(0)
            halve(1)
            first_x()
        begin = 0 if g == 0 else g * group - 1
        end = planes - 1 if g == planes // group - 1 else (g + 1) * group - 1
        sums = lax.fori_loop(begin, end, lambda x, s: plane(x, s, True), sums)
    sums = plane(planes - 1, sums, True)
    plane(planes, sums, False)

    def total(values):
        return jnp.sum(jnp.sum(values, axis=1, keepdims=True), axis=0, keepdims=True)

    square, product, bb = [total(values) for values in sums]
    some = square > 0.0
    mu = jnp.where(some, product / jnp.where(some, square, 1.0), 0.0)

    def take_off(x, carry):
        for i in range(strips + 1):
            rows = pl.ds(8 + 8 * i, 8)
            image[x, rows, :] = image[x, rows, :] - mu * field[x + 1, rows, :]
        return carry

    lax.fori_loop(0, planes + 1, take_off, 0)
    each = where_ref.shape[0] // planes

    def rest(x, sums):
        vv, bv, vav = sums
        copy_rows(table, picks, where_ref, x * each, each)
        for i in range(strips):
            at = 8 + 8 * i
            rows, out = pl.ds(at, 8), pl.ds(8 * i, 8)
            v = image[x, rows, :]
            d_x = v - image[x + 1, rows, :]
            d_y = v - image[x, pl.ds(at + 1, 8), :]
            d_z = v - pltpu.roll(v, depth - 1, 1)
            sv = store[x, rows, :] * v
            vv = vv + v * v
            bv = bv + (sv * field[x + 1, rows, :] + flow_x[x, out, :] * d_x) + (
                flow_y[x, out, :] * d_y + flow_z[x, out, :] * d_z
            )
            vav = vav + (sv * v + con_x[x, out, :] * (d_x * d_x)) + (
                con_y[x, out, :] * (d_y * d_y) + con_z[x, out, :] * (d_z * d_z)
            )
        return vv, bv, vav

    vv, bv, vav = [total(values) for values in lax.fori_loop(0, planes, rest, (zero, zero, zero))]

    chunks = dest_ref.shape[0]
    dest = dest_ref[...]
    columns = columns_ref[...]
    owner = lax.broadcasted_iota(jnp.int32, (LANES, LANES), 0)
    for c in range(chunks):
        span = pl.ds(c * LANES, LANES)
        owners[:, span] = onehot(owner == dest[c : c + 1, :])
        value = columns[:, chunks + c : chunks + c + 1] * pick_lane(
            picks[span, :], columns[:, 2 * chunks + c : 2 * chunks + c + 1]
        )
        spread[span, :] = grouped_pieces(value, columns[:, c : c + 1])
    summed = jnp.dot(owners[...], spread[...], preferred_element_type=jnp.float32)
    sent = sent_in_ref[...] + join_groups(summed, 2)
    place = lax.broadcasted_iota(jnp.int32, sent.shape, 1)
    for n, scalar in enumerate((square, mu, vv, bb, bv, vav)):
        sent = jnp.where(place == 3 * SLOTS + n, scalar, sent)
    sent_ref[...] = sent


def apply_flow(where, even, dest, columns, sent, cells, subs, source, permeability, storage):
    planes, height, depth = source.shape
    count = where.shape[0]
    chunks = count // LANES
    vmem = pl.BlockSpec(memory_space=pltpu.VMEM)
    smem = pl.BlockSpec(memory_space=pltpu.SMEM)
    hbm = pl.BlockSpec(memory_space=pl.ANY)
    wide = lambda n: pltpu.VMEM((n, height + 16, depth), jnp.float32)
    block = pltpu.VMEM((planes, height, depth), jnp.float32)
    return pl.pallas_call(
        image_kernel,
        out_shape=(
            jax.ShapeDtypeStruct(source.shape, jnp.float32),
            jax.ShapeDtypeStruct((LANES, LANES), jnp.float32),
        ),
        in_specs=[smem, smem] + [vmem] * 7 + [hbm] * 3,
        out_specs=(vmem, vmem),
        scratch_shapes=[
            wide(planes + 3),
            wide(planes + 3),
            wide(planes + 1),
            wide(planes + 1),
        ]
        + [block] * 6
        + [
            pltpu.VMEM((height + 16, depth), jnp.float32),
            pltpu.VMEM((2 * planes * height, LANES), jnp.float32),
            pltpu.VMEM((count, LANES), jnp.float32),
            pltpu.VMEM((LANES, count), jnp.bfloat16),
            pltpu.VMEM((count, LANES), jnp.bfloat16),
            pltpu.SemaphoreType.DMA((3 * planes // 8,)),
        ],
        compiler_params=pltpu.CompilerParams(vmem_limit_bytes=36 * 2**20),
        name="image",
    )(where, even, dest.reshape(chunks, LANES), columns, sent, *cells, *subs, source, permeability, storage)


def final_kernel(
    steps,
    kind_ref,
    got_ref,
    tectonic_ref,
    yield_ref,
    free_ref,
    matrix_ref,
    source_ref,
    image_ref,
    pressure_ref,
    slip_ref,
    wide,
    tall,
    turned,
    rows,
):
    patches, unknowns = tectonic_ref.shape
    tiles = unknowns // LANES
    got = got_ref[...]
    across = got.T
    scal = [across[3 * SLOTS + i : 3 * SLOTS + i + 1, :] for i in range(6)]
    square, mu, rest_sq, bb, bv, vv = scal

    def total(row):
        return jnp.sum(row, axis=1, keepdims=True)

    norm = total(square)
    alpha = norm / total(bb)
    part = 1.0 - alpha * mu
    edge = part * jnp.sqrt(square)
    norm_next = total(edge * edge + alpha * alpha * rest_sq)
    beta = norm_next / norm
    part = part + beta
    curve = total(part * part * bb - 2.0 * part * alpha * bv + alpha * alpha * vv)
    alpha_next = norm_next / curve
    on_source = alpha + alpha_next * (1.0 + beta)
    on_image = -alpha_next * alpha

    count = got.shape[0]
    code = got[:, :SLOTS].astype(jnp.int32)
    code_across = across[:SLOTS].astype(jnp.int32)
    terms = on_source * across[SLOTS : 2 * SLOTS] + on_image * across[2 * SLOTS : 3 * SLOTS]
    pieces = split3(terms)
    lane = lax.broadcasted_iota(jnp.int32, (count, LANES), 1)
    high = lax.broadcasted_iota(jnp.int32, (8 * tiles, count), 0)
    low_code = code & (LANES - 1)
    high_code = code_across >> 7
    for slot in range(SLOTS):
        span = pl.ds(slot * count, count)
        wide[span, :] = (lane == low_code[:, slot : slot + 1]).astype(jnp.float32).astype(jnp.bfloat16)
        here = high == high_code[slot : slot + 1, :]
        for index, piece in enumerate(pieces):
            tall[pl.ds(index * 8 * tiles, 8 * tiles), span] = jnp.where(
                here, piece[slot : slot + 1, :], 0.0
            ).astype(jnp.bfloat16)
    summed = jnp.dot(tall[...], wide[...], preferred_element_type=jnp.float32)
    summed = summed[: 8 * tiles] + summed[8 * tiles : 16 * tiles] + summed[16 * tiles :]
    loads = jnp.concatenate([summed[8 * t : 8 * t + 8] for t in range(tiles)], axis=1)
    fault_load = tectonic_ref[...] + loads[:patches]

    for x in range(0, source_ref.shape[0], 4):
        pressure_ref[x : x + 4] = on_source[None] * source_ref[x : x + 4] + on_image[None] * image_ref[x : x + 4]

    piece_row = lax.broadcasted_iota(jnp.int32, (16, patches * LANES), 0)
    piece_lane = lax.broadcasted_iota(jnp.int32, (16, patches * LANES), 1)
    choose = onehot((piece_row & 3) == (piece_lane >> 7))

    def times_matrix(vector):
        pieces = jnp.concatenate([*split3(vector), jnp.zeros_like(vector)], axis=0)
        turned[...] = jnp.dot(
            pieces.T.astype(jnp.bfloat16), choose, preferred_element_type=jnp.float32
        )
        group = 8

        def body(i, sums):
            sums = list(sums)
            for g in range(group):
                start = pl.multiple_of(i * (8 * group), 8 * group) + 8 * g
                for p in range(patches):
                    spread = turned[pl.ds(start, 8), p * LANES : (p + 1) * LANES]
                    sums[p] = sums[p] + matrix_ref[p, pl.ds(start, 8), :] * jnp.concatenate(
                        [spread] * tiles, axis=1
                    )
            return tuple(sums)

        zero = jnp.zeros((8, unknowns), jnp.float32)
        sums = lax.fori_loop(0, unknowns // (8 * group), body, (zero,) * patches)
        for p in range(patches):
            rows[p : p + 1, :] = jnp.sum(sums[p], axis=0, keepdims=True)
        return rows[:patches, :]

    def mean(values):
        return jnp.sum(values, axis=1, keepdims=True) * (1.0 / unknowns)

    limit = yield_ref[...]
    row = lax.broadcasted_iota(jnp.int32, (patches, unknowns), 0)
    slip_now = None
    previous = None
    previous_image = None
    for iteration in range(steps):
        if iteration == 0:
            gradient = -fault_load
        else:
            gradient = times_matrix(slip_now) - fault_load
        free_part = jnp.where(free_ref[iteration] == 1, gradient, 0.0)
        kind = jnp.zeros((patches, unknowns), jnp.int32)
        for p in range(patches):
            kind = jnp.where(row == p, kind_ref[iteration, p], kind)
        conjugate = free_part
        if iteration > 0:
            conjugacy = mean(free_part * previous_image) / (mean(previous * previous_image) + 1e-06)
            conjugate = free_part - conjugacy * previous
        direction = jnp.where(
            kind == 0, conjugate, jnp.where(kind == 1, gradient - free_part, gradient)
        )
        image_vec = times_matrix(direction)
        step_length = mean(gradient * direction) / (mean(direction * image_vec) + 1e-06)
        moved = -step_length * direction if iteration == 0 else slip_now - step_length * direction
        slip_now = jnp.clip(moved, -limit, limit)
        previous = direction
        previous_image = image_vec
    slip_ref[...] = slip_now


def finish(got, tectonic_load, yield_limit, free_mask, step_kind, patch_matrix, source, image):
    patches, unknowns = tectonic_load.shape
    tiles = unknowns // LANES
    count = got.shape[0]
    vmem = pl.BlockSpec(memory_space=pltpu.VMEM)
    return pl.pallas_call(
        functools.partial(final_kernel, step_kind.shape[0]),
        out_shape=(
            jax.ShapeDtypeStruct(source.shape, jnp.float32),
            jax.ShapeDtypeStruct(tectonic_load.shape, jnp.float32),
        ),
        in_specs=[pl.BlockSpec(memory_space=pltpu.SMEM)] + [vmem] * 7,
        out_specs=(vmem, vmem),
        scratch_shapes=[
            pltpu.VMEM((SLOTS * count, LANES), jnp.bfloat16),
            pltpu.VMEM((24 * tiles, SLOTS * count), jnp.bfloat16),
            pltpu.VMEM((unknowns, patches * LANES), jnp.float32),
            pltpu.VMEM((8, unknowns), jnp.float32),
        ],
        compiler_params=pltpu.CompilerParams(vmem_limit_bytes=20 * 2**20),
        name="finish",
    )(step_kind, got, tectonic_load, yield_limit, free_mask, patch_matrix, source, image)


def swap_pairs(head, tail, axis):
    count = lax.axis_size(axis)
    even = lax.axis_index(axis) % 2 == 0
    first = [(i, i ^ 1) for i in range(count)]
    second = [(i, i + 1) for i in range(1, count - 1, 2)]
    second = second + [(j, i) for i, j in second]
    return (
        lax.ppermute(jnp.where(even, tail, head), axis, first),
        lax.ppermute(jnp.where(even, head, tail), axis, second),
    )


def load_code(face_dof, unknowns):
    patch, unknown = face_dof // unknowns, face_dof % unknowns
    return ((unknown // LANES * 8 + patch) * LANES + unknown % LANES).astype(jnp.float32)


def on_device(
    source,
    permeability,
    storage,
    face_cell,
    face_dest,
    face_dof,
    face_weight,
    tectonic_load,
    patch_matrix,
    yield_limit,
    free_mask,
    step_kind,
):
    planes, height, depth = source.shape
    even_cell = lax.axis_index("cell") % 2 == 0
    even_sub = lax.axis_index("sub") % 2 == 0
    head = jnp.stack([source[0], source[1], permeability[0], permeability[1], storage[0]])
    tail = jnp.stack([source[-1], source[-2], permeability[-1], permeability[-2], storage[-1]])
    cells = swap_pairs(head, tail, "cell")
    before = jnp.where(even_cell, cells[1], cells[0])
    after = jnp.where(even_cell, cells[0], cells[1])

    def rows(near, far):
        def column(array, plane, y):
            return jnp.concatenate([before[plane, y][None], array[:, y], after[plane, y][None]])

        return jnp.stack(
            [
                column(source, 0, near),
                column(source, 0, far),
                column(permeability, 2, near),
                column(permeability, 2, far),
                column(storage, 4, near),
            ]
        )

    subs = swap_pairs(rows(0, 1), rows(height - 1, height - 2), "sub")

    where = (face_cell >> 7) % 2 * (planes * height) + (face_cell >> 8)
    dest = face_dest[:, 0]
    sent, columns = faces(
        source, where, face_cell & (LANES - 1), dest, load_code(face_dof, tectonic_load.shape[1]), face_weight
    )
    even = jnp.stack([even_cell, even_sub]).astype(jnp.int32)
    image, sent = apply_flow(where, even, dest, columns, sent, cells, subs, source, permeability, storage)
    got = lax.all_to_all(sent, AXES, 0, 0, tiled=True)
    pressure_change, slip = finish(
        got, tectonic_load, yield_limit, free_mask, step_kind, patch_matrix, source, image
    )
    return (pressure_change, slip)


def solution(mesh):
    return jax.shard_map(
        on_device,
        mesh=mesh,
        in_specs=(
            P("cell", "sub", None),
            P("cell", "sub", None),
            P("cell", "sub", None),
            P(("cell", "sub")),
            P(("cell", "sub"), None),
            P(("cell", "sub")),
            P(("cell", "sub")),
            P(("cell", "sub"), None),
            P(("cell", "sub"), None, None),
            P(("cell", "sub"), None),
            P(None, ("cell", "sub"), None),
            P(None, ("cell", "sub")),
        ),
        out_specs=(P("cell", "sub", None), P(("cell", "sub"), None)),
        check_vma=False,
    )
```

```python
import functools

import jax
import jax.numpy as jnp
from jax import lax
from jax.experimental import pallas as pl
from jax.experimental.pallas import tpu as pltpu
from jax.sharding import PartitionSpec as P

SLOTS = 32
AXES = ("cell", "sub")
LANES = 128
EDGES = 61 * 2**20
INSIDE = 46 * 2**20
UNROLL = 2


def split3(values):
    first = values.astype(jnp.bfloat16).astype(jnp.float32)
    left = values - first
    second = left.astype(jnp.bfloat16).astype(jnp.float32)
    return first, second, left - second


def onehot(values):
    return values.astype(jnp.float32).astype(jnp.bfloat16)


def dot(left, right):
    return jnp.dot(left, right, preferred_element_type=jnp.float32)


def pieces_of(values):
    return jnp.concatenate([piece.astype(jnp.bfloat16) for piece in split3(values)], axis=1)


def spread_columns(columns, chunks):
    shape = (columns.shape[1], chunks * LANES)
    take = lax.broadcasted_iota(jnp.int32, shape, 0) % chunks == lax.broadcasted_iota(jnp.int32, shape, 1) // LANES
    return dot(columns, onehot(take))


def sum_lanes(values):
    return dot(pieces_of(values), jnp.ones((3 * LANES, LANES), jnp.bfloat16))


def grouped_pieces(value, slots):
    lane = lax.broadcasted_iota(jnp.int32, value.shape, 1)
    first, second, third = split3(value)
    piece = jnp.where(lane < SLOTS, first, jnp.where(lane < 2 * SLOTS, second, third))
    return jnp.where(slots > 0.0, piece, 0.0).astype(jnp.bfloat16)


def join_groups(summed, group):
    lane = lax.broadcasted_iota(jnp.int32, summed.shape, 1)
    joined = summed + pltpu.roll(summed, LANES - SLOTS, 1) + pltpu.roll(summed, LANES - 2 * SLOTS, 1)
    if group:
        joined = pltpu.roll(joined, group * SLOTS, 1)
    return jnp.where((lane >= group * SLOTS) & (lane < (group + 1) * SLOTS), joined, 0.0)


def copy_rows(table, picks, where_ref, first, count):
    for j in range(count):
        picks[pl.ds(first + j, 1), :] = table[pl.ds(where_ref[first + j], 1), :]


def faces_kernel(
    where_ref,
    dest_ref,
    code_ref,
    weight_ref,
    lane_ref,
    source_ref,
    sent_ref,
    slots_ref,
    picker_ref,
    table,
    picks,
    owners,
    spread,
    sems,
):
    chunks = dest_ref.shape[0]
    rows = source_ref.shape[0]
    halves = [
        pltpu.make_async_copy(
            source_ref.at[:, pl.ds(t * LANES, LANES)], table.at[pl.ds(t * rows, rows), :], sems.at[t]
        )
        for t in range(2)
    ]
    for half in halves:
        half.start()
    dest = dest_ref[...].astype(jnp.float32)
    lane = lax.broadcasted_iota(jnp.int32, (LANES, LANES), 1)
    row = lax.broadcasted_iota(jnp.int32, (LANES, LANES), 0)
    lower = onehot(lane < row)
    lane_number = lane.astype(jnp.float32)
    row_number = row.astype(jnp.float32)
    ones = jnp.ones((LANES, LANES), jnp.bfloat16)
    dest_spread = spread_columns(dest.T.astype(jnp.bfloat16), chunks)
    lane_spread = spread_columns(lane_ref[...].astype(jnp.float32).T.astype(jnp.bfloat16), chunks)
    weight_spread = spread_columns(pieces_of(weight_ref[...].T), chunks)
    code_spread = spread_columns(pieces_of(code_ref[...].T), chunks)
    start = jnp.zeros((1, LANES), jnp.float32)
    for c in range(chunks):
        span = pl.ds(c * LANES, LANES)
        cut = slice(c * LANES, (c + 1) * LANES)
        named = (lane_number == dest_spread[:, cut]).astype(jnp.float32)
        ahead = dot(lower, named.astype(jnp.bfloat16))
        rank = dot((named * (ahead + start)).astype(jnp.bfloat16), ones)
        start = start + jnp.sum(named, axis=0, keepdims=True)
        here = ((lane & (SLOTS - 1)).astype(jnp.float32) == rank) & (lane < 3 * SLOTS)
        slots = here.astype(jnp.float32)
        slots_ref[:, span] = slots.astype(jnp.bfloat16)
        picker_ref[:, span] = jnp.where(lane_number == lane_spread[:, cut], weight_spread[:, cut], 0.0)
        owners[:, span] = onehot(row_number == dest[c : c + 1, :])
        spread[span, :LANES] = grouped_pieces(code_spread[:, cut], slots)
    for half in halves:
        half.wait()

    def gather(i, carry):
        copy_rows(table, picks, where_ref, i * 64, 64)
        return carry

    lax.fori_loop(0, chunks * LANES // 64, gather, 0)
    for c in range(chunks):
        span = pl.ds(c * LANES, LANES)
        value = sum_lanes(picks[span, :] * picker_ref[:, span])
        spread[span, LANES:] = grouped_pieces(value, slots_ref[:, span].astype(jnp.float32))
    summed = dot(owners[...], spread[...])
    sent_ref[...] = join_groups(summed[:, :LANES], 0) + join_groups(summed[:, LANES:], 1)


def faces(source, where, lane, dest, code, weight):
    count = where.shape[0]
    chunks = count // LANES
    rows = source.shape[0] * source.shape[1]
    vmem = pl.BlockSpec(memory_space=pltpu.VMEM)
    cut = lambda values: values.reshape(chunks, LANES)
    return pl.pallas_call(
        faces_kernel,
        out_shape=(
            jax.ShapeDtypeStruct((LANES, LANES), jnp.float32),
            jax.ShapeDtypeStruct((LANES, count), jnp.bfloat16),
            jax.ShapeDtypeStruct((LANES, count), jnp.float32),
        ),
        in_specs=[pl.BlockSpec(memory_space=pltpu.SMEM)] + [vmem] * 4 + [pl.BlockSpec(memory_space=pltpu.HBM)],
        out_specs=(vmem, vmem, vmem),
        scratch_shapes=[
            pltpu.VMEM((2 * rows, LANES), jnp.float32),
            pltpu.VMEM((count, LANES), jnp.float32),
            pltpu.VMEM((LANES, count), jnp.bfloat16),
            pltpu.VMEM((count, 2 * LANES), jnp.bfloat16),
            pltpu.SemaphoreType.DMA((2,)),
        ],
        compiler_params=pltpu.CompilerParams(vmem_limit_bytes=12 * 2**20),
        name="faces",
    )(where, cut(dest), cut(code), cut(weight), cut(lane), source.reshape(rows, source.shape[2]))


def image_kernel(
    source_ref,
    perm_ref,
    storage_ref,
    image_ref,
    con_x_ref,
    con_y_ref,
    con_z_ref,
    sums_ref,
    first_ref,
    second_ref,
    field,
    half,
    store,
    carry_x,
    sems,
):
    planes, height, depth = source_ref.shape
    strips = height // 8
    group = 8
    copies = []
    for g in range(planes // group):
        span = pl.ds(g * group, group)
        for n, (array, held) in enumerate(((source_ref, field), (perm_ref, half), (storage_ref, store))):
            copies.append(pltpu.make_async_copy(array.at[span], held.at[span], sems.at[3 * g + n]))
    for copy in copies:
        copy.start()
    lane = lax.broadcasted_iota(jnp.int32, (8, depth), 1)
    row = lax.broadcasted_iota(jnp.int32, (8, depth), 0)
    zero = jnp.zeros((8, depth), jnp.float32)

    even = is_even("sub")
    for out in (first_ref, second_ref):
        for n in range(len(WANTED)):
            out[n, 0:8, :] = zero
            out[n, planes : planes + 8, :] = zero

    def send_rows(x):
        for k, out in enumerate((first_ref, second_ref)):
            at_end = even if k == 0 else 1 - even
            for n, (f, deep) in enumerate(WANTED):
                row = deep + at_end * (height - 1 - 2 * deep)
                out[n, pl.ds(x + 1, 1), :] = (field, half, store)[f][x, pl.ds(row, 1), :]

    def plane(x, sums, last):
        if not last:
            send_rows(x + 1)
            half[x + 1] = half_of(half[x + 1])
        square, product = sums
        last_y = zero
        for i in range(strips):
            at = 8 * i
            rows = pl.ds(at, 8)
            b, h = field[x, rows, :], half[x, rows, :]
            if i + 1 < strips:
                b_y, h_y = field[x, pl.ds(at + 1, 8), :], half[x, pl.ds(at + 1, 8), :]
                c_y = 1.0 / (h + h_y)
            else:
                b_y, h_y = pltpu.roll(b, 7, 0), pltpu.roll(h, 7, 0)
                c_y = jnp.where(row == 7, 0.0, 1.0 / (h + h_y))
            c_z = jnp.where(lane == depth - 1, 0.0, 1.0 / (h + pltpu.roll(h, depth - 1, 1)))
            f_y, f_z = c_y * (b - b_y), c_z * (b - pltpu.roll(b, depth - 1, 1))
            came_y = pltpu.roll(jnp.where(row == 7, last_y, f_y), 1, 0)
            last_y = f_y
            w = store[x, rows, :] * b + (f_y - came_y) + (f_z - pltpu.roll(f_z, 1, 1)) - carry_x[rows, :]
            if last:
                c_x = zero
            else:
                c_x = 1.0 / (h + half[x + 1, rows, :])
                f_x = c_x * (b - field[x + 1, rows, :])
                carry_x[rows, :] = f_x
                w = w + f_x
            image_ref[x, rows, :] = w
            con_x_ref[x, rows, :] = c_x
            con_y_ref[x, rows, :] = c_y
            con_z_ref[x, rows, :] = c_z
            square = square + b * b
            product = product + b * w
        return square, product

    sums = (zero, zero)
    chunks = planes // group
    for copy in copies[:3]:
        copy.wait()
    send_rows(0)
    half[0] = half_of(half[0])
    carry_x[...] = jnp.zeros_like(carry_x)
    for g in range(chunks):
        for copy in copies[3 * g + 3 : 3 * g + 6]:
            copy.wait()
        runs = group // UNROLL if g + 1 < chunks else group // UNROLL - 1

        def run(n, sums):
            for u in range(UNROLL):
                sums = plane(g * group + n * UNROLL + u, sums, False)
            return sums

        sums = lax.fori_loop(0, runs, run, sums)
    for x in range(planes - UNROLL, planes - 1):
        sums = plane(x, sums, False)
    square, product = plane(planes - 1, sums, True)
    sums_ref[0] = square
    sums_ref[1] = product


def half_of(perm):
    return 0.5 / jnp.maximum(perm, 1e-30)


def image_inside(source, permeability, storage):
    planes, height, depth = source.shape
    vmem = pl.BlockSpec(memory_space=pltpu.VMEM)
    block = jax.ShapeDtypeStruct(source.shape, jnp.float32)
    held = pltpu.VMEM(source.shape, jnp.float32)
    line = jax.ShapeDtypeStruct((5, planes + 8, depth), jnp.float32)
    return pl.pallas_call(
        image_kernel,
        out_shape=(block,) * 4 + (jax.ShapeDtypeStruct((2, 8, depth), jnp.float32), line, line),
        in_specs=[pl.BlockSpec(memory_space=pl.ANY)] * 3,
        out_specs=(vmem,) * 7,
        scratch_shapes=[
            held,
            held,
            held,
            pltpu.VMEM((height, depth), jnp.float32),
            pltpu.SemaphoreType.DMA((3 * planes // 8,)),
        ],
        compiler_params=pltpu.CompilerParams(vmem_limit_bytes=INSIDE),
        name="image",
    )(source, permeability, storage)


def norms_kernel(
    where_ref,
    dest_ref,
    slots_ref,
    picker_ref,
    sent_in_ref,
    side_first_ref,
    side_second_ref,
    cell_first_ref,
    cell_second_ref,
    line_first_ref,
    line_second_ref,
    sub_first_ref,
    sub_second_ref,
    part_ref,
    con_x_ref,
    con_y_ref,
    con_z_ref,
    sums_ref,
    source_ref,
    storage_ref,
    image_ref,
    sent_ref,
    rest,
    flows,
    lines,
    table,
    picks,
    owners,
    spread,
):
    planes, height, depth = source_ref.shape
    strips = height // 8
    even_cell = is_even("cell") == 1
    even_sub = is_even("sub") == 1

    def total(values):
        return jnp.sum(jnp.sum(values, axis=1, keepdims=True), axis=0, keepdims=True)

    def conduct(one, other):
        return 1.0 / (half_of(one) + half_of(other))

    def along_depth(b, k):
        lane = lax.broadcasted_iota(jnp.int32, b.shape, 1)
        flow = conduct(k, pltpu.roll(k, depth - 1, 1)) * (b - pltpu.roll(b, depth - 1, 1))
        flow = jnp.where(lane == depth - 1, 0.0, flow)
        return flow - pltpu.roll(flow, 1, 1)

    def cell_side(n):
        one, two = cell_first_ref[n], cell_second_ref[n]
        return jnp.where(even_cell, two, one), jnp.where(even_cell, one, two)

    def own_side(n):
        one, two = side_first_ref[n], side_second_ref[n]
        return jnp.where(even_cell, two, one), jnp.where(even_cell, one, two)

    b_lo, b_hi = cell_side(0)
    b_far = cell_side(1)[1]
    k_lo, k_hi = cell_side(2)
    k_far = cell_side(3)[1]
    s_hi = cell_side(4)[1]
    b_head, b_tail = own_side(0)
    k_head, k_tail = own_side(2)
    con_hi = conduct(k_tail, k_hi)
    flow_lo = conduct(k_lo, k_head) * (b_lo - b_head)
    flow_hi = con_hi * (b_tail - b_hi)

    def sub_side(n):
        one, two = sub_first_ref[n], sub_second_ref[n]
        return jnp.where(even_sub, two, one), jnp.where(even_sub, one, two)

    def own_line(n):
        one, two = line_first_ref[n], line_second_ref[n]
        return jnp.where(even_sub, two, one), jnp.where(even_sub, one, two)

    by_lo, by_hi = sub_side(0)
    by_far = sub_side(1)[1]
    ky_lo, ky_hi = sub_side(2)
    ky_far = sub_side(3)[1]
    sy_hi = sub_side(4)[1]
    by_head, by_tail = own_line(0)
    ky_head, ky_tail = own_line(2)
    cony_hi = conduct(ky_tail, ky_hi)
    flowy_lo = conduct(ky_lo, ky_head) * (by_lo - by_head)
    flowy_hi = cony_hi * (by_tail - by_hi)
    count = by_lo.shape[0]
    number = lax.broadcasted_iota(jnp.int32, by_lo.shape, 0)
    inside = (number >= 1) & (number <= planes)

    row = lax.broadcasted_iota(jnp.int32, b_hi.shape, 0)
    flow = conduct(k_hi, pltpu.roll(k_hi, height - 1, 0)) * (b_hi - pltpu.roll(b_hi, height - 1, 0))
    flow = jnp.where(row == height - 1, flowy_hi[planes + 1 : planes + 2], flow)
    came = jnp.where(row == 0, flowy_lo[planes + 1 : planes + 2], pltpu.roll(flow, 1, 0))
    w_hi = s_hi * b_hi + (conduct(k_hi, k_far) * (b_hi - b_far) - flow_hi) + (flow - came)
    w_hi = w_hi + along_depth(b_hi, k_hi)

    flow = conduct(ky_hi, pltpu.roll(ky_hi, count - 1, 0)) * (by_hi - pltpu.roll(by_hi, count - 1, 0))
    wy_hi = sy_hi * by_hi + (conduct(ky_hi, ky_far) * (by_hi - by_far) - flowy_hi)
    wy_hi = wy_hi + (flow - pltpu.roll(flow, 1, 0)) + along_depth(by_hi, ky_hi)

    def rows_total(values):
        return total(jnp.where(inside, values, 0.0))

    square = total(sums_ref[0])
    lower = total(flow_lo * b_head) + rows_total(flowy_lo * by_head)
    product = total(sums_ref[1]) - lower + total(flow_hi * b_tail) + rows_total(flowy_hi * by_tail)
    bb = product - total(flow_hi * b_hi) - rows_total(flowy_hi * by_hi) + lower
    some = square > 0.0
    mu = jnp.where(some, product / jnp.where(some, square, 1.0), 0.0)

    flows[0] = flowy_lo
    flows[1] = flowy_hi
    lines[...] = jnp.zeros_like(lines)
    strip_row = lax.broadcasted_iota(jnp.int32, (8, depth), 0)

    def complete(x, extra):
        for i in range(strips):
            rows = pl.ds(8 * i, 8)
            w = part_ref[x, rows, :]
            if extra is not None:
                w = w + extra[8 * i : 8 * i + 8]
            if i == 0:
                w = w - jnp.where(strip_row == 0, flows[0, pl.ds(x + 1, 1), :], 0.0)
            if i == strips - 1:
                w = w + jnp.where(strip_row == 7, flows[1, pl.ds(x + 1, 1), :], 0.0)
            image_ref[x, rows, :] = w
            for t in range(2):
                table[pl.ds(pl.multiple_of((t * planes + x) * height, 8) + 8 * i, 8), :] = w[
                    :, t * LANES : (t + 1) * LANES
                ]
            v = w - mu * source_ref[x, rows, :]
            rest[x, rows, :] = v
            if i == 0:
                lines[0, pl.ds(x + 1, 1), :] = v[0:1]
            if i == strips - 1:
                lines[1, pl.ds(x + 1, 1), :] = v[7:8]

    complete(0, -flow_lo)

    def middle(x, carry):
        complete(x, None)
        return carry

    lax.fori_loop(1, planes - 1, middle, 0)
    complete(planes - 1, flow_hi)
    v_hi = w_hi - mu * b_hi
    vy_hi = wy_hi - mu * by_hi
    rest[planes] = v_hi

    each = where_ref.shape[0] // planes

    def measure(x, sums):
        vv, vav = sums
        copy_rows(table, picks, where_ref, x * each, each)
        for i in range(strips):
            rows = pl.ds(8 * i, 8)
            v = rest[x, rows, :]
            d_x = v - rest[x + 1, rows, :]
            if i + 1 < strips:
                d_y = v - rest[x, pl.ds(8 * i + 1, 8), :]
            else:
                d_y = v - pltpu.roll(v, 7, 0)
            d_z = v - pltpu.roll(v, depth - 1, 1)
            squared = v * v
            vv = vv + squared
            vav = vav + (storage_ref[x, rows, :] * squared + con_x_ref[x, rows, :] * (d_x * d_x)) + (
                con_y_ref[x, rows, :] * (d_y * d_y) + con_z_ref[x, rows, :] * (d_z * d_z)
            )
        return vv, vav

    zero = jnp.zeros((8, depth), jnp.float32)
    vv, vav = [total(values) for values in lax.fori_loop(0, planes, measure, (zero, zero))]
    v_head, v_tail = rest[0], rest[planes - 1]
    vy_head, vy_tail = lines[0], lines[1]
    bv = vv - total(flow_hi * v_hi) - rows_total(flowy_hi * vy_hi)
    bv = bv + total(flow_lo * v_head) + rows_total(flowy_lo * vy_head)
    vav = vav + total(con_hi * ((v_tail - v_hi) * (v_tail - v_hi)))
    vav = vav + rows_total(cony_hi * ((vy_tail - vy_hi) * (vy_tail - vy_hi)))

    chunks = dest_ref.shape[0]
    dest = dest_ref[...]
    owner = lax.broadcasted_iota(jnp.int32, (LANES, LANES), 0)
    for c in range(chunks):
        span = pl.ds(c * LANES, LANES)
        owners[:, span] = onehot(owner == dest[c : c + 1, :])
        value = sum_lanes(picks[span, :] * picker_ref[:, span])
        spread[span, :] = grouped_pieces(value, slots_ref[:, span].astype(jnp.float32))
    summed = dot(owners[...], spread[...])
    sent = sent_in_ref[...] + join_groups(summed, 2)
    place = lax.broadcasted_iota(jnp.int32, sent.shape, 1)
    for n, scalar in enumerate((square, mu, vv, bb, bv, vav)):
        sent = jnp.where(place == 3 * SLOTS + n, scalar, sent)
    sent_ref[...] = sent


def norms(where, dest, marks, sides, cells, lines, subs, inner, source, storage):
    planes, height, depth = source.shape
    count = where.shape[0]
    chunks = count // LANES
    vmem = pl.BlockSpec(memory_space=pltpu.VMEM)
    smem = pl.BlockSpec(memory_space=pltpu.SMEM)
    line = pltpu.VMEM((2,) + lines[0].shape[1:], jnp.float32)
    operands = (dest.reshape(chunks, LANES), *marks, *sides, *cells, *lines, *subs, *inner, source, storage)
    return pl.pallas_call(
        norms_kernel,
        out_shape=(
            jax.ShapeDtypeStruct(source.shape, jnp.float32),
            jax.ShapeDtypeStruct((LANES, LANES), jnp.float32),
        ),
        in_specs=[smem] + [vmem] * len(operands),
        out_specs=(vmem, vmem),
        scratch_shapes=[
            pltpu.VMEM((planes + 1, height, depth), jnp.float32),
            line,
            line,
            pltpu.VMEM((2 * planes * height, LANES), jnp.float32),
            pltpu.VMEM((count, LANES), jnp.float32),
            pltpu.VMEM((LANES, count), jnp.bfloat16),
            pltpu.VMEM((count, LANES), jnp.bfloat16),
        ],
        compiler_params=pltpu.CompilerParams(vmem_limit_bytes=16 * 2**20),
        name="norms",
    )(where, *operands)


def final_kernel(
    steps,
    kind_ref,
    got_ref,
    tectonic_ref,
    yield_ref,
    free_ref,
    matrix_ref,
    source_ref,
    image_ref,
    pressure_ref,
    slip_ref,
    pressure,
    wide,
    tall,
    turned,
    rows,
    sem,
):
    patches, unknowns = tectonic_ref.shape
    tiles = unknowns // LANES
    got = got_ref[...]
    across = got.T
    scal = [across[3 * SLOTS + i : 3 * SLOTS + i + 1, :] for i in range(6)]
    square, mu, rest_sq, bb, bv, vv = scal

    def total(row):
        return jnp.sum(row, axis=1, keepdims=True)

    norm = total(square)
    alpha = norm / total(bb)
    part = 1.0 - alpha * mu
    edge = part * jnp.sqrt(square)
    norm_next = total(edge * edge + alpha * alpha * rest_sq)
    beta = norm_next / norm
    part = part + beta
    curve = total(part * part * bb - 2.0 * part * alpha * bv + alpha * alpha * vv)
    alpha_next = norm_next / curve
    on_source = alpha + alpha_next * (1.0 + beta)
    on_image = -alpha_next * alpha

    count = got.shape[0]
    code = got[:, :SLOTS].astype(jnp.int32)
    code_across = across[:SLOTS].astype(jnp.int32)
    terms = on_source * across[SLOTS : 2 * SLOTS] + on_image * across[2 * SLOTS : 3 * SLOTS]
    pieces = split3(terms)
    lane = lax.broadcasted_iota(jnp.int32, (count, LANES), 1)
    high = lax.broadcasted_iota(jnp.int32, (8 * tiles, count), 0)
    low_code = code & (LANES - 1)
    high_code = code_across >> 7
    for slot in range(SLOTS):
        span = pl.ds(slot * count, count)
        wide[span, :] = (lane == low_code[:, slot : slot + 1]).astype(jnp.float32).astype(jnp.bfloat16)
        here = high == high_code[slot : slot + 1, :]
        for index, piece in enumerate(pieces):
            tall[pl.ds(index * 8 * tiles, 8 * tiles), span] = jnp.where(
                here, piece[slot : slot + 1, :], 0.0
            ).astype(jnp.bfloat16)
    summed = jnp.dot(tall[...], wide[...], preferred_element_type=jnp.float32)
    summed = summed[: 8 * tiles] + summed[8 * tiles : 16 * tiles] + summed[16 * tiles :]
    loads = jnp.concatenate([summed[8 * t : 8 * t + 8] for t in range(tiles)], axis=1)
    fault_load = tectonic_ref[...] + loads[:patches]

    for x in range(0, source_ref.shape[0], 4):
        pressure[x : x + 4] = on_source[None] * source_ref[x : x + 4] + on_image[None] * image_ref[x : x + 4]

    leaving = pltpu.make_async_copy(pressure, pressure_ref, sem)
    leaving.start()

    piece_row = lax.broadcasted_iota(jnp.int32, (16, patches * LANES), 0)
    piece_lane = lax.broadcasted_iota(jnp.int32, (16, patches * LANES), 1)
    choose = onehot((piece_row & 3) == (piece_lane >> 7))

    def times_matrix(vector):
        pieces = jnp.concatenate([*split3(vector), jnp.zeros_like(vector)], axis=0)
        turned[...] = jnp.dot(
            pieces.T.astype(jnp.bfloat16), choose, preferred_element_type=jnp.float32
        )
        group = 16

        def body(i, sums):
            sums = list(sums)
            for g in range(group):
                start = pl.multiple_of(i * (8 * group), 8 * group) + 8 * g
                for p in range(patches):
                    spread = turned[pl.ds(start, 8), p * LANES : (p + 1) * LANES]
                    sums[p] = sums[p] + matrix_ref[p, pl.ds(start, 8), :] * jnp.concatenate(
                        [spread] * tiles, axis=1
                    )
            return tuple(sums)

        zero = jnp.zeros((8, unknowns), jnp.float32)
        sums = lax.fori_loop(0, unknowns // (8 * group), body, (zero,) * patches)
        for p in range(patches):
            rows[p : p + 1, :] = jnp.sum(sums[p], axis=0, keepdims=True)
        return rows[:patches, :]

    def mean(values):
        return jnp.sum(values, axis=1, keepdims=True) * (1.0 / unknowns)

    limit = yield_ref[...]
    row = lax.broadcasted_iota(jnp.int32, (patches, unknowns), 0)
    slip_now = None
    previous = None
    previous_image = None
    for iteration in range(steps):
        if iteration == 0:
            gradient = -fault_load
        else:
            gradient = times_matrix(slip_now) - fault_load
        free_part = jnp.where(free_ref[iteration] == 1, gradient, 0.0)
        kind = jnp.zeros((patches, unknowns), jnp.int32)
        for p in range(patches):
            kind = jnp.where(row == p, kind_ref[iteration, p], kind)
        conjugate = free_part
        if iteration > 0:
            conjugacy = mean(free_part * previous_image) / curved
            conjugate = free_part - conjugacy * previous
        direction = jnp.where(
            kind == 0, conjugate, jnp.where(kind == 1, gradient - free_part, gradient)
        )
        image_vec = times_matrix(direction)
        curved = mean(direction * image_vec) + 1e-06
        step_length = mean(gradient * direction) / curved
        moved = -step_length * direction if iteration == 0 else slip_now - step_length * direction
        slip_now = jnp.clip(moved, -limit, limit)
        previous = direction
        previous_image = image_vec
    slip_ref[...] = slip_now
    leaving.wait()


def finish(got, tectonic_load, yield_limit, free_mask, step_kind, patch_matrix, source, image):
    patches, unknowns = tectonic_load.shape
    tiles = unknowns // LANES
    count = got.shape[0]
    vmem = pl.BlockSpec(memory_space=pltpu.VMEM)
    return pl.pallas_call(
        functools.partial(final_kernel, step_kind.shape[0]),
        out_shape=(
            jax.ShapeDtypeStruct(source.shape, jnp.float32),
            jax.ShapeDtypeStruct(tectonic_load.shape, jnp.float32),
        ),
        in_specs=[pl.BlockSpec(memory_space=pltpu.SMEM)] + [vmem] * 7,
        out_specs=(pl.BlockSpec(memory_space=pl.ANY), vmem),
        scratch_shapes=[
            pltpu.VMEM(source.shape, jnp.float32),
            pltpu.VMEM((SLOTS * count, LANES), jnp.bfloat16),
            pltpu.VMEM((24 * tiles, SLOTS * count), jnp.bfloat16),
            pltpu.VMEM((unknowns, patches * LANES), jnp.float32),
            pltpu.VMEM((8, unknowns), jnp.float32),
            pltpu.SemaphoreType.DMA,
        ],
        compiler_params=pltpu.CompilerParams(vmem_limit_bytes=20 * 2**20),
        name="finish",
    )(step_kind, got, tectonic_load, yield_limit, free_mask, patch_matrix, source, image)


def is_even(axis):
    return (lax.axis_index(axis) + 1) % 2


WANTED = ((0, 0), (0, 1), (1, 0), (1, 1), (2, 0))


def edges_kernel(source_ref, perm_ref, storage_ref, first_ref, second_ref, sems):
    planes = source_ref.shape[0]
    fields = (source_ref, perm_ref, storage_ref)
    even = is_even("cell")
    copies = []
    for n, (f, deep) in enumerate(WANTED):
        for k, out in enumerate((first_ref, second_ref)):
            at_end = even if k == 0 else 1 - even
            plane = deep + at_end * (planes - 1 - 2 * deep)
            copies.append(pltpu.make_async_copy(fields[f].at[plane], out.at[n], sems.at[2 * n + k]))
    for copy in copies:
        copy.start()
    for copy in copies:
        copy.wait()


def edges(source, permeability, storage):
    vmem = pl.BlockSpec(memory_space=pltpu.VMEM)
    side = jax.ShapeDtypeStruct((5,) + source.shape[1:], jnp.float32)
    return pl.pallas_call(
        edges_kernel,
        out_shape=(side, side),
        in_specs=[pl.BlockSpec(memory_space=pl.ANY)] * 3,
        out_specs=(vmem,) * 2,
        scratch_shapes=[pltpu.SemaphoreType.DMA((10,))],
        compiler_params=pltpu.CompilerParams(vmem_limit_bytes=EDGES),
        name="edges",
    )(source, permeability, storage)


def corners_kernel(one_ref, two_ref, first_in_ref, second_in_ref, first_ref, second_ref):
    height = one_ref.shape[1]
    last = first_ref.shape[1] - 7
    even_cell = is_even("cell") == 1
    even_sub = is_even("sub")
    first_ref[...] = first_in_ref[...]
    second_ref[...] = second_in_ref[...]
    for k, out in enumerate((first_ref, second_ref)):
        at_end = even_sub if k == 0 else 1 - even_sub
        row = pl.ds(at_end * (height - 1), 1)
        for n in (0, 2):
            one, two = one_ref[n, row, :], two_ref[n, row, :]
            out[n, 0:1, :] = jnp.where(even_cell, two, one)
            out[n, last : last + 1, :] = jnp.where(even_cell, one, two)


def corners(cells, lines):
    vmem = pl.BlockSpec(memory_space=pltpu.VMEM)
    line = jax.ShapeDtypeStruct(lines[0].shape, jnp.float32)
    return pl.pallas_call(
        corners_kernel,
        out_shape=(line, line),
        in_specs=[vmem] * 4,
        out_specs=(vmem, vmem),
        compiler_params=pltpu.CompilerParams(vmem_limit_bytes=8 * 2**20),
        name="corners",
    )(*cells, *lines)


def swap_pairs(first_sent, second_sent, axis):
    count = lax.axis_size(axis)
    first = [(i, i ^ 1) for i in range(count)]
    second = [(i, i + 1) for i in range(1, count - 1, 2)]
    second = second + [(j, i) for i, j in second]
    return lax.ppermute(first_sent, axis, first), lax.ppermute(second_sent, axis, second)


def load_code(face_dof, unknowns):
    patch, unknown = face_dof // unknowns, face_dof % unknowns
    return ((unknown // LANES * 8 + patch) * LANES + unknown % LANES).astype(jnp.float32)


def on_device(
    source,
    permeability,
    storage,
    face_cell,
    face_dest,
    face_dof,
    face_weight,
    tectonic_load,
    patch_matrix,
    yield_limit,
    free_mask,
    step_kind,
):
    planes, height, depth = source.shape
    sides = edges(source, permeability, storage)
    cells = swap_pairs(*sides, "cell")
    *inner, first, second = image_inside(source, permeability, storage)
    lines = corners(cells, (first, second))
    subs = swap_pairs(*lines, "sub")

    where = (face_cell >> 7) % 2 * (planes * height) + (face_cell >> 8)
    dest = face_dest[:, 0]
    sent, slots, picker = faces(
        source, where, face_cell & (LANES - 1), dest, load_code(face_dof, tectonic_load.shape[1]), face_weight
    )
    image, sent = norms(
        where, dest, (slots, picker, sent), sides, cells, lines, subs, inner, source, storage
    )
    got = lax.all_to_all(sent, AXES, 0, 0, tiled=True)
    pressure_change, slip = finish(
        got, tectonic_load, yield_limit, free_mask, step_kind, patch_matrix, source, image
    )
    return (pressure_change, slip)


def solution(mesh):
    return jax.shard_map(
        on_device,
        mesh=mesh,
        in_specs=(
            P("cell", "sub", None),
            P("cell", "sub", None),
            P("cell", "sub", None),
            P(("cell", "sub")),
            P(("cell", "sub"), None),
            P(("cell", "sub")),
            P(("cell", "sub")),
            P(("cell", "sub"), None),
            P(("cell", "sub"), None, None),
            P(("cell", "sub"), None),
            P(None, ("cell", "sub"), None),
            P(None, ("cell", "sub")),
        ),
        out_specs=(P("cell", "sub", None), P(("cell", "sub"), None)),
        check_vma=False,
    )
```

```python
import functools

import jax
import jax.numpy as jnp
from jax import lax
from jax.experimental import pallas as pl
from jax.experimental.pallas import tpu as pltpu
from jax.sharding import PartitionSpec as P

SLOTS = 32
AXES = ("cell", "sub")
LANES = 128
EDGES = 61 * 2**20
INSIDE = 46 * 2**20
UNROLL = 2


def split3(values):
    first = values.astype(jnp.bfloat16).astype(jnp.float32)
    left = values - first
    second = left.astype(jnp.bfloat16).astype(jnp.float32)
    return first, second, left - second


def onehot(values):
    return values.astype(jnp.float32).astype(jnp.bfloat16)


def dot(left, right):
    return jnp.dot(left, right, preferred_element_type=jnp.float32)


def pieces_of(values):
    return jnp.concatenate([piece.astype(jnp.bfloat16) for piece in split3(values)], axis=1)


def spread_columns(columns, chunks):
    shape = (columns.shape[1], chunks * LANES)
    take = lax.broadcasted_iota(jnp.int32, shape, 0) % chunks == lax.broadcasted_iota(jnp.int32, shape, 1) // LANES
    return dot(columns, onehot(take))


def sum_lanes(values):
    return dot(pieces_of(values), jnp.ones((3 * LANES, LANES), jnp.bfloat16))


def grouped_pieces(value, slots):
    lane = lax.broadcasted_iota(jnp.int32, value.shape, 1)
    first, second, third = split3(value)
    piece = jnp.where(lane < SLOTS, first, jnp.where(lane < 2 * SLOTS, second, third))
    return jnp.where(slots > 0.0, piece, 0.0).astype(jnp.bfloat16)


def join_groups(summed, group):
    lane = lax.broadcasted_iota(jnp.int32, summed.shape, 1)
    joined = summed + pltpu.roll(summed, LANES - SLOTS, 1) + pltpu.roll(summed, LANES - 2 * SLOTS, 1)
    if group:
        joined = pltpu.roll(joined, group * SLOTS, 1)
    return jnp.where((lane >= group * SLOTS) & (lane < (group + 1) * SLOTS), joined, 0.0)


def copy_rows(table, picks, where_ref, first, count):
    for j in range(count):
        picks[pl.ds(first + j, 1), :] = table[pl.ds(where_ref[first + j], 1), :]


def slots_kernel(
    dest_ref,
    code_ref,
    weight_ref,
    lane_ref,
    source_ref,
    sent_ref,
    slots_ref,
    picker_ref,
    table_ref,
    owners,
    spread,
    sems,
):
    chunks = dest_ref.shape[0]
    rows = source_ref.shape[0]
    halves = [
        pltpu.make_async_copy(
            source_ref.at[:, pl.ds(t * LANES, LANES)], table_ref.at[pl.ds(t * rows, rows), :], sems.at[t]
        )
        for t in range(2)
    ]
    for half in halves:
        half.start()
    dest = dest_ref[...].astype(jnp.float32)
    lane = lax.broadcasted_iota(jnp.int32, (LANES, LANES), 1)
    row = lax.broadcasted_iota(jnp.int32, (LANES, LANES), 0)
    lower = onehot(lane < row)
    lane_number = lane.astype(jnp.float32)
    row_number = row.astype(jnp.float32)
    ones = jnp.ones((LANES, LANES), jnp.bfloat16)
    dest_spread = spread_columns(dest.T.astype(jnp.bfloat16), chunks)
    lane_spread = spread_columns(lane_ref[...].astype(jnp.float32).T.astype(jnp.bfloat16), chunks)
    weight_spread = spread_columns(pieces_of(weight_ref[...].T), chunks)
    code_spread = spread_columns(pieces_of(code_ref[...].T), chunks)
    start = jnp.zeros((1, LANES), jnp.float32)
    for c in range(chunks):
        span = pl.ds(c * LANES, LANES)
        cut = slice(c * LANES, (c + 1) * LANES)
        named = (lane_number == dest_spread[:, cut]).astype(jnp.float32)
        ahead = dot(lower, named.astype(jnp.bfloat16))
        rank = dot((named * (ahead + start)).astype(jnp.bfloat16), ones)
        start = start + jnp.sum(named, axis=0, keepdims=True)
        here = ((lane & (SLOTS - 1)).astype(jnp.float32) == rank) & (lane < 3 * SLOTS)
        slots = here.astype(jnp.float32)
        slots_ref[:, span] = slots.astype(jnp.bfloat16)
        picker_ref[:, span] = jnp.where(lane_number == lane_spread[:, cut], weight_spread[:, cut], 0.0)
        owners[:, span] = onehot(row_number == dest[c : c + 1, :])
        spread[span, :] = grouped_pieces(code_spread[:, cut], slots)
    sent_ref[...] = join_groups(dot(owners[...], spread[...]), 0)
    for half in halves:
        half.wait()


def values_kernel(
    where_ref, dest_ref, slots_ref, picker_ref, sent_in_ref, table_ref, sent_ref, picks, owners, spread
):
    chunks = dest_ref.shape[0]

    def gather(i, carry):
        copy_rows(table_ref, picks, where_ref, i * 64, 64)
        return carry

    lax.fori_loop(0, chunks * LANES // 64, gather, 0)
    face_values(dest_ref, slots_ref, picker_ref, picks, owners, spread)
    sent_ref[...] = sent_in_ref[...] + join_groups(dot(owners[...], spread[...]), 1)


def face_values(dest_ref, slots_ref, picker_ref, picks, owners, spread):
    dest = dest_ref[...]
    owner = lax.broadcasted_iota(jnp.int32, (LANES, LANES), 0)
    for c in range(dest.shape[0]):
        span = pl.ds(c * LANES, LANES)
        owners[:, span] = onehot(owner == dest[c : c + 1, :])
        value = sum_lanes(picks[span, :] * picker_ref[:, span])
        spread[span, :] = grouped_pieces(value, slots_ref[:, span].astype(jnp.float32))


def face_slots(source, lane, dest, code, weight):
    count = dest.shape[0]
    chunks = count // LANES
    rows = source.shape[0] * source.shape[1]
    vmem = pl.BlockSpec(memory_space=pltpu.VMEM)
    cut = lambda values: values.reshape(chunks, LANES)
    return pl.pallas_call(
        slots_kernel,
        out_shape=(
            jax.ShapeDtypeStruct((LANES, LANES), jnp.float32),
            jax.ShapeDtypeStruct((LANES, count), jnp.bfloat16),
            jax.ShapeDtypeStruct((LANES, count), jnp.float32),
            jax.ShapeDtypeStruct((2 * rows, LANES), jnp.float32),
        ),
        in_specs=[vmem] * 4 + [pl.BlockSpec(memory_space=pl.ANY)],
        out_specs=(vmem,) * 4,
        scratch_shapes=[
            pltpu.VMEM((LANES, count), jnp.bfloat16),
            pltpu.VMEM((count, LANES), jnp.bfloat16),
            pltpu.SemaphoreType.DMA((2,)),
        ],
        compiler_params=pltpu.CompilerParams(vmem_limit_bytes=8 * 2**20),
        name="slots",
    )(cut(dest), cut(code), cut(weight), cut(lane), source.reshape(rows, source.shape[2]))


def add_values(where, dest, slots, picker, sent, table):
    count = where.shape[0]
    vmem = pl.BlockSpec(memory_space=pltpu.VMEM)
    return pl.pallas_call(
        values_kernel,
        out_shape=jax.ShapeDtypeStruct((LANES, LANES), jnp.float32),
        in_specs=[pl.BlockSpec(memory_space=pltpu.SMEM)] + [vmem] * 5,
        out_specs=vmem,
        scratch_shapes=[
            pltpu.VMEM((count, LANES), jnp.float32),
            pltpu.VMEM((LANES, count), jnp.bfloat16),
            pltpu.VMEM((count, LANES), jnp.bfloat16),
        ],
        compiler_params=pltpu.CompilerParams(vmem_limit_bytes=8 * 2**20),
        name="values",
    )(where, dest.reshape(count // LANES, LANES), slots, picker, sent, table)


def image_kernel(
    source_ref,
    perm_ref,
    storage_ref,
    image_ref,
    con_x_ref,
    con_y_ref,
    con_z_ref,
    sums_ref,
    first_ref,
    second_ref,
    field,
    half,
    store,
    carry_x,
    sems,
):
    planes, height, depth = source_ref.shape
    strips = height // 8
    group = 8
    copies = []
    for g in range(planes // group):
        span = pl.ds(g * group, group)
        for n, (array, held) in enumerate(((source_ref, field), (perm_ref, half), (storage_ref, store))):
            copies.append(pltpu.make_async_copy(array.at[span], held.at[span], sems.at[3 * g + n]))
    for copy in copies:
        copy.start()
    lane = lax.broadcasted_iota(jnp.int32, (8, depth), 1)
    row = lax.broadcasted_iota(jnp.int32, (8, depth), 0)
    zero = jnp.zeros((8, depth), jnp.float32)

    even = is_even("sub")
    for out in (first_ref, second_ref):
        for n in range(len(WANTED)):
            out[n, 0:8, :] = zero
            out[n, planes : planes + 8, :] = zero

    def send_rows(x):
        for k, out in enumerate((first_ref, second_ref)):
            at_end = even if k == 0 else 1 - even
            for n, (f, deep) in enumerate(WANTED):
                row = deep + at_end * (height - 1 - 2 * deep)
                out[n, pl.ds(x + 1, 1), :] = (field, half, store)[f][x, pl.ds(row, 1), :]

    def plane(x, sums, last):
        if not last:
            send_rows(x + 1)
            half[x + 1] = half_of(half[x + 1])
        square, product = sums
        last_y = zero
        for i in range(strips):
            at = 8 * i
            rows = pl.ds(at, 8)
            b, h = field[x, rows, :], half[x, rows, :]
            if i + 1 < strips:
                b_y, h_y = field[x, pl.ds(at + 1, 8), :], half[x, pl.ds(at + 1, 8), :]
                c_y = 1.0 / (h + h_y)
            else:
                b_y, h_y = pltpu.roll(b, 7, 0), pltpu.roll(h, 7, 0)
                c_y = jnp.where(row == 7, 0.0, 1.0 / (h + h_y))
            c_z = jnp.where(lane == depth - 1, 0.0, 1.0 / (h + pltpu.roll(h, depth - 1, 1)))
            f_y, f_z = c_y * (b - b_y), c_z * (b - pltpu.roll(b, depth - 1, 1))
            came_y = pltpu.roll(jnp.where(row == 7, last_y, f_y), 1, 0)
            last_y = f_y
            w = store[x, rows, :] * b + (f_y - came_y) + (f_z - pltpu.roll(f_z, 1, 1)) - carry_x[rows, :]
            if last:
                c_x = zero
            else:
                c_x = 1.0 / (h + half[x + 1, rows, :])
                f_x = c_x * (b - field[x + 1, rows, :])
                carry_x[rows, :] = f_x
                w = w + f_x
            image_ref[x, rows, :] = w
            con_x_ref[x, rows, :] = c_x
            con_y_ref[x, rows, :] = c_y
            con_z_ref[x, rows, :] = c_z
            square = square + b * b
            product = product + b * w
        return square, product

    sums = (zero, zero)
    chunks = planes // group
    for copy in copies[:3]:
        copy.wait()
    send_rows(0)
    half[0] = half_of(half[0])
    carry_x[...] = jnp.zeros_like(carry_x)
    for g in range(chunks):
        for copy in copies[3 * g + 3 : 3 * g + 6]:
            copy.wait()
        runs = group // UNROLL if g + 1 < chunks else group // UNROLL - 1

        def run(n, sums):
            for u in range(UNROLL):
                sums = plane(g * group + n * UNROLL + u, sums, False)
            return sums

        sums = lax.fori_loop(0, runs, run, sums)
    for x in range(planes - UNROLL, planes - 1):
        sums = plane(x, sums, False)
    square, product = plane(planes - 1, sums, True)
    sums_ref[0] = square
    sums_ref[1] = product


def half_of(perm):
    return 0.5 / jnp.maximum(perm, 1e-30)


def image_inside(source, permeability, storage):
    planes, height, depth = source.shape
    vmem = pl.BlockSpec(memory_space=pltpu.VMEM)
    block = jax.ShapeDtypeStruct(source.shape, jnp.float32)
    held = pltpu.VMEM(source.shape, jnp.float32)
    line = jax.ShapeDtypeStruct((5, planes + 8, depth), jnp.float32)
    return pl.pallas_call(
        image_kernel,
        out_shape=(block,) * 4 + (jax.ShapeDtypeStruct((2, 8, depth), jnp.float32), line, line),
        in_specs=[pl.BlockSpec(memory_space=pl.ANY)] * 3,
        out_specs=(vmem,) * 7,
        scratch_shapes=[
            held,
            held,
            held,
            pltpu.VMEM((height, depth), jnp.float32),
            pltpu.SemaphoreType.DMA((3 * planes // 8,)),
        ],
        compiler_params=pltpu.CompilerParams(vmem_limit_bytes=INSIDE),
        name="image",
    )(source, permeability, storage)


def norms_kernel(
    where_ref,
    dest_ref,
    slots_ref,
    picker_ref,
    sent_in_ref,
    side_first_ref,
    side_second_ref,
    cell_first_ref,
    cell_second_ref,
    line_first_ref,
    line_second_ref,
    sub_first_ref,
    sub_second_ref,
    part_ref,
    con_x_ref,
    con_y_ref,
    con_z_ref,
    sums_ref,
    source_ref,
    storage_ref,
    image_ref,
    sent_ref,
    rest,
    flows,
    lines,
    table,
    picks,
    owners,
    spread,
):
    planes, height, depth = source_ref.shape
    strips = height // 8
    even_cell = is_even("cell") == 1
    even_sub = is_even("sub") == 1

    def total(values):
        return jnp.sum(jnp.sum(values, axis=1, keepdims=True), axis=0, keepdims=True)

    def conduct(one, other):
        return 1.0 / (half_of(one) + half_of(other))

    def along_depth(b, k):
        lane = lax.broadcasted_iota(jnp.int32, b.shape, 1)
        flow = conduct(k, pltpu.roll(k, depth - 1, 1)) * (b - pltpu.roll(b, depth - 1, 1))
        flow = jnp.where(lane == depth - 1, 0.0, flow)
        return flow - pltpu.roll(flow, 1, 1)

    def cell_side(n):
        one, two = cell_first_ref[n], cell_second_ref[n]
        return jnp.where(even_cell, two, one), jnp.where(even_cell, one, two)

    def own_side(n):
        one, two = side_first_ref[n], side_second_ref[n]
        return jnp.where(even_cell, two, one), jnp.where(even_cell, one, two)

    b_lo, b_hi = cell_side(0)
    b_far = cell_side(1)[1]
    k_lo, k_hi = cell_side(2)
    k_far = cell_side(3)[1]
    s_hi = cell_side(4)[1]
    b_head, b_tail = own_side(0)
    k_head, k_tail = own_side(2)
    con_hi = conduct(k_tail, k_hi)
    flow_lo = conduct(k_lo, k_head) * (b_lo - b_head)
    flow_hi = con_hi * (b_tail - b_hi)

    def sub_side(n):
        one, two = sub_first_ref[n], sub_second_ref[n]
        return jnp.where(even_sub, two, one), jnp.where(even_sub, one, two)

    def own_line(n):
        one, two = line_first_ref[n], line_second_ref[n]
        return jnp.where(even_sub, two, one), jnp.where(even_sub, one, two)

    by_lo, by_hi = sub_side(0)
    by_far = sub_side(1)[1]
    ky_lo, ky_hi = sub_side(2)
    ky_far = sub_side(3)[1]
    sy_hi = sub_side(4)[1]
    by_head, by_tail = own_line(0)
    ky_head, ky_tail = own_line(2)
    cony_hi = conduct(ky_tail, ky_hi)
    flowy_lo = conduct(ky_lo, ky_head) * (by_lo - by_head)
    flowy_hi = cony_hi * (by_tail - by_hi)
    count = by_lo.shape[0]
    number = lax.broadcasted_iota(jnp.int32, by_lo.shape, 0)
    inside = (number >= 1) & (number <= planes)

    row = lax.broadcasted_iota(jnp.int32, b_hi.shape, 0)
    flow = conduct(k_hi, pltpu.roll(k_hi, height - 1, 0)) * (b_hi - pltpu.roll(b_hi, height - 1, 0))
    flow = jnp.where(row == height - 1, flowy_hi[planes + 1 : planes + 2], flow)
    came = jnp.where(row == 0, flowy_lo[planes + 1 : planes + 2], pltpu.roll(flow, 1, 0))
    w_hi = s_hi * b_hi + (conduct(k_hi, k_far) * (b_hi - b_far) - flow_hi) + (flow - came)
    w_hi = w_hi + along_depth(b_hi, k_hi)

    flow = conduct(ky_hi, pltpu.roll(ky_hi, count - 1, 0)) * (by_hi - pltpu.roll(by_hi, count - 1, 0))
    wy_hi = sy_hi * by_hi + (conduct(ky_hi, ky_far) * (by_hi - by_far) - flowy_hi)
    wy_hi = wy_hi + (flow - pltpu.roll(flow, 1, 0)) + along_depth(by_hi, ky_hi)

    def rows_total(values):
        return total(jnp.where(inside, values, 0.0))

    square = total(sums_ref[0])
    lower = total(flow_lo * b_head) + rows_total(flowy_lo * by_head)
    product = total(sums_ref[1]) - lower + total(flow_hi * b_tail) + rows_total(flowy_hi * by_tail)
    bb = product - total(flow_hi * b_hi) - rows_total(flowy_hi * by_hi) + lower
    some = square > 0.0
    mu = jnp.where(some, product / jnp.where(some, square, 1.0), 0.0)

    flows[0] = flowy_lo
    flows[1] = flowy_hi
    lines[...] = jnp.zeros_like(lines)
    strip_row = lax.broadcasted_iota(jnp.int32, (8, depth), 0)

    def complete(x, extra):
        for i in range(strips):
            rows = pl.ds(8 * i, 8)
            w = part_ref[x, rows, :]
            if extra is not None:
                w = w + extra[8 * i : 8 * i + 8]
            if i == 0:
                w = w - jnp.where(strip_row == 0, flows[0, pl.ds(x + 1, 1), :], 0.0)
            if i == strips - 1:
                w = w + jnp.where(strip_row == 7, flows[1, pl.ds(x + 1, 1), :], 0.0)
            image_ref[x, rows, :] = w
            for t in range(2):
                table[pl.ds(pl.multiple_of((t * planes + x) * height, 8) + 8 * i, 8), :] = w[
                    :, t * LANES : (t + 1) * LANES
                ]
            v = w - mu * source_ref[x, rows, :]
            rest[x, rows, :] = v
            if i == 0:
                lines[0, pl.ds(x + 1, 1), :] = v[0:1]
            if i == strips - 1:
                lines[1, pl.ds(x + 1, 1), :] = v[7:8]

    complete(0, -flow_lo)

    def middle(x, carry):
        complete(x, None)
        return carry

    lax.fori_loop(0, planes // 2 - 1, lambda n, c: middle(2 * n + 2, middle(2 * n + 1, c)), 0)
    complete(planes - 1, flow_hi)
    v_hi = w_hi - mu * b_hi
    vy_hi = wy_hi - mu * by_hi
    rest[planes] = v_hi

    each = where_ref.shape[0] // planes

    def measure(x, sums):
        vv, vav = sums
        copy_rows(table, picks, where_ref, x * each, each)
        for i in range(strips):
            rows = pl.ds(8 * i, 8)
            v = rest[x, rows, :]
            d_x = v - rest[x + 1, rows, :]
            if i + 1 < strips:
                d_y = v - rest[x, pl.ds(8 * i + 1, 8), :]
            else:
                d_y = v - pltpu.roll(v, 7, 0)
            d_z = v - pltpu.roll(v, depth - 1, 1)
            squared = v * v
            vv = vv + squared
            vav = vav + (storage_ref[x, rows, :] * squared + con_x_ref[x, rows, :] * (d_x * d_x)) + (
                con_y_ref[x, rows, :] * (d_y * d_y) + con_z_ref[x, rows, :] * (d_z * d_z)
            )
        return vv, vav

    zero = jnp.zeros((8, depth), jnp.float32)
    sums = lax.fori_loop(0, planes // 2, lambda n, s: measure(2 * n + 1, measure(2 * n, s)), (zero, zero))
    vv, vav = [total(values) for values in sums]
    v_head, v_tail = rest[0], rest[planes - 1]
    vy_head, vy_tail = lines[0], lines[1]
    bv = vv - total(flow_hi * v_hi) - rows_total(flowy_hi * vy_hi)
    bv = bv + total(flow_lo * v_head) + rows_total(flowy_lo * vy_head)
    vav = vav + total(con_hi * ((v_tail - v_hi) * (v_tail - v_hi)))
    vav = vav + rows_total(cony_hi * ((vy_tail - vy_hi) * (vy_tail - vy_hi)))

    face_values(dest_ref, slots_ref, picker_ref, picks, owners, spread)
    summed = dot(owners[...], spread[...])
    sent = sent_in_ref[...] + join_groups(summed, 2)
    place = lax.broadcasted_iota(jnp.int32, sent.shape, 1)
    for n, scalar in enumerate((square, mu, vv, bb, bv, vav)):
        sent = jnp.where(place == 3 * SLOTS + n, scalar, sent)
    sent_ref[...] = sent


def norms(where, dest, marks, sides, cells, lines, subs, inner, source, storage):
    planes, height, depth = source.shape
    count = where.shape[0]
    chunks = count // LANES
    vmem = pl.BlockSpec(memory_space=pltpu.VMEM)
    smem = pl.BlockSpec(memory_space=pltpu.SMEM)
    line = pltpu.VMEM((2,) + lines[0].shape[1:], jnp.float32)
    operands = (dest.reshape(chunks, LANES), *marks, *sides, *cells, *lines, *subs, *inner, source, storage)
    return pl.pallas_call(
        norms_kernel,
        out_shape=(
            jax.ShapeDtypeStruct(source.shape, jnp.float32),
            jax.ShapeDtypeStruct((LANES, LANES), jnp.float32),
        ),
        in_specs=[smem] + [vmem] * len(operands),
        out_specs=(vmem, vmem),
        scratch_shapes=[
            pltpu.VMEM((planes + 1, height, depth), jnp.float32),
            line,
            line,
            pltpu.VMEM((2 * planes * height, LANES), jnp.float32),
            pltpu.VMEM((count, LANES), jnp.float32),
            pltpu.VMEM((LANES, count), jnp.bfloat16),
            pltpu.VMEM((count, LANES), jnp.bfloat16),
        ],
        compiler_params=pltpu.CompilerParams(vmem_limit_bytes=12 * 2**20),
        name="norms",
    )(where, *operands)


def final_kernel(
    steps,
    kind_ref,
    got_ref,
    tectonic_ref,
    yield_ref,
    free_ref,
    matrix_ref,
    source_ref,
    image_ref,
    pressure_ref,
    slip_ref,
    pressure,
    wide,
    tall,
    turned,
    rows,
    sem,
):
    patches, unknowns = tectonic_ref.shape
    tiles = unknowns // LANES
    got = got_ref[...]
    across = got.T
    scal = [across[3 * SLOTS + i : 3 * SLOTS + i + 1, :] for i in range(6)]
    square, mu, rest_sq, bb, bv, vv = scal

    def total(row):
        return jnp.sum(row, axis=1, keepdims=True)

    norm = total(square)
    alpha = norm / total(bb)
    part = 1.0 - alpha * mu
    edge = part * jnp.sqrt(square)
    norm_next = total(edge * edge + alpha * alpha * rest_sq)
    beta = norm_next / norm
    part = part + beta
    curve = total(part * part * bb - 2.0 * part * alpha * bv + alpha * alpha * vv)
    alpha_next = norm_next / curve
    on_source = alpha + alpha_next * (1.0 + beta)
    on_image = -alpha_next * alpha

    count = got.shape[0]
    code = got[:, :SLOTS].astype(jnp.int32)
    code_across = across[:SLOTS].astype(jnp.int32)
    terms = on_source * across[SLOTS : 2 * SLOTS] + on_image * across[2 * SLOTS : 3 * SLOTS]
    pieces = split3(terms)
    lane = lax.broadcasted_iota(jnp.int32, (count, LANES), 1)
    high = lax.broadcasted_iota(jnp.int32, (8 * tiles, count), 0)
    low_code = code & (LANES - 1)
    high_code = code_across >> 7
    for slot in range(SLOTS):
        span = pl.ds(slot * count, count)
        wide[span, :] = (lane == low_code[:, slot : slot + 1]).astype(jnp.float32).astype(jnp.bfloat16)
        here = high == high_code[slot : slot + 1, :]
        for index, piece in enumerate(pieces):
            tall[pl.ds(index * 8 * tiles, 8 * tiles), span] = jnp.where(
                here, piece[slot : slot + 1, :], 0.0
            ).astype(jnp.bfloat16)
    summed = jnp.dot(tall[...], wide[...], preferred_element_type=jnp.float32)
    summed = summed[: 8 * tiles] + summed[8 * tiles : 16 * tiles] + summed[16 * tiles :]
    loads = jnp.concatenate([summed[8 * t : 8 * t + 8] for t in range(tiles)], axis=1)
    fault_load = tectonic_ref[...] + loads[:patches]

    for x in range(0, source_ref.shape[0], 4):
        pressure[x : x + 4] = on_source[None] * source_ref[x : x + 4] + on_image[None] * image_ref[x : x + 4]

    leaving = pltpu.make_async_copy(pressure, pressure_ref, sem)
    leaving.start()

    piece_row = lax.broadcasted_iota(jnp.int32, (16, patches * LANES), 0)
    piece_lane = lax.broadcasted_iota(jnp.int32, (16, patches * LANES), 1)
    choose = onehot((piece_row & 3) == (piece_lane >> 7))

    def times_matrix(vector):
        pieces = jnp.concatenate([*split3(vector), jnp.zeros_like(vector)], axis=0)
        turned[...] = jnp.dot(
            pieces.T.astype(jnp.bfloat16), choose, preferred_element_type=jnp.float32
        )
        group = 16

        def body(i, sums):
            sums = list(sums)
            for g in range(group):
                start = pl.multiple_of(i * (8 * group), 8 * group) + 8 * g
                for p in range(patches):
                    spread = turned[pl.ds(start, 8), p * LANES : (p + 1) * LANES]
                    sums[p] = sums[p] + matrix_ref[p, pl.ds(start, 8), :] * jnp.concatenate(
                        [spread] * tiles, axis=1
                    )
            return tuple(sums)

        zero = jnp.zeros((8, unknowns), jnp.float32)
        sums = lax.fori_loop(0, unknowns // (8 * group), body, (zero,) * patches)
        for p in range(patches):
            rows[p : p + 1, :] = jnp.sum(sums[p], axis=0, keepdims=True)
        return rows[:patches, :]

    def mean(values):
        return jnp.sum(values, axis=1, keepdims=True) * (1.0 / unknowns)

    limit = yield_ref[...]
    row = lax.broadcasted_iota(jnp.int32, (patches, unknowns), 0)
    slip_now = None
    previous = None
    previous_image = None
    for iteration in range(steps):
        if iteration == 0:
            gradient = -fault_load
        else:
            gradient = times_matrix(slip_now) - fault_load
        free_part = jnp.where(free_ref[iteration] == 1, gradient, 0.0)
        kind = jnp.zeros((patches, unknowns), jnp.int32)
        for p in range(patches):
            kind = jnp.where(row == p, kind_ref[iteration, p], kind)
        conjugate = free_part
        if iteration > 0:
            conjugacy = mean(free_part * previous_image) / curved
            conjugate = free_part - conjugacy * previous
        direction = jnp.where(
            kind == 0, conjugate, jnp.where(kind == 1, gradient - free_part, gradient)
        )
        image_vec = times_matrix(direction)
        curved = mean(direction * image_vec) + 1e-06
        step_length = mean(gradient * direction) / curved
        moved = -step_length * direction if iteration == 0 else slip_now - step_length * direction
        slip_now = jnp.clip(moved, -limit, limit)
        previous = direction
        previous_image = image_vec
    slip_ref[...] = slip_now
    leaving.wait()


def finish(got, tectonic_load, yield_limit, free_mask, step_kind, patch_matrix, source, image):
    patches, unknowns = tectonic_load.shape
    tiles = unknowns // LANES
    count = got.shape[0]
    vmem = pl.BlockSpec(memory_space=pltpu.VMEM)
    return pl.pallas_call(
        functools.partial(final_kernel, step_kind.shape[0]),
        out_shape=(
            jax.ShapeDtypeStruct(source.shape, jnp.float32),
            jax.ShapeDtypeStruct(tectonic_load.shape, jnp.float32),
        ),
        in_specs=[pl.BlockSpec(memory_space=pltpu.SMEM)] + [vmem] * 7,
        out_specs=(pl.BlockSpec(memory_space=pl.ANY), vmem),
        scratch_shapes=[
            pltpu.VMEM(source.shape, jnp.float32),
            pltpu.VMEM((SLOTS * count, LANES), jnp.bfloat16),
            pltpu.VMEM((24 * tiles, SLOTS * count), jnp.bfloat16),
            pltpu.VMEM((unknowns, patches * LANES), jnp.float32),
            pltpu.VMEM((8, unknowns), jnp.float32),
            pltpu.SemaphoreType.DMA,
        ],
        compiler_params=pltpu.CompilerParams(vmem_limit_bytes=20 * 2**20),
        name="finish",
    )(step_kind, got, tectonic_load, yield_limit, free_mask, patch_matrix, source, image)


def is_even(axis):
    return (lax.axis_index(axis) + 1) % 2


WANTED = ((0, 0), (0, 1), (1, 0), (1, 1), (2, 0))


def edges_kernel(source_ref, perm_ref, storage_ref, first_ref, second_ref, sems):
    planes = source_ref.shape[0]
    fields = (source_ref, perm_ref, storage_ref)
    even = is_even("cell")
    copies = []
    for n, (f, deep) in enumerate(WANTED):
        for k, out in enumerate((first_ref, second_ref)):
            at_end = even if k == 0 else 1 - even
            plane = deep + at_end * (planes - 1 - 2 * deep)
            copies.append(pltpu.make_async_copy(fields[f].at[plane], out.at[n], sems.at[2 * n + k]))
    for copy in copies:
        copy.start()
    for copy in copies:
        copy.wait()


def edges(source, permeability, storage):
    vmem = pl.BlockSpec(memory_space=pltpu.VMEM)
    side = jax.ShapeDtypeStruct((5,) + source.shape[1:], jnp.float32)
    return pl.pallas_call(
        edges_kernel,
        out_shape=(side, side),
        in_specs=[pl.BlockSpec(memory_space=pl.ANY)] * 3,
        out_specs=(vmem,) * 2,
        scratch_shapes=[pltpu.SemaphoreType.DMA((10,))],
        compiler_params=pltpu.CompilerParams(vmem_limit_bytes=EDGES),
        name="edges",
    )(source, permeability, storage)


def corners_kernel(one_ref, two_ref, first_in_ref, second_in_ref, after_ref, first_ref, second_ref):
    height = one_ref.shape[1]
    last = first_ref.shape[1] - 7
    even_cell = is_even("cell") == 1
    even_sub = is_even("sub")
    first_ref[...] = first_in_ref[...]
    second_ref[...] = second_in_ref[...]
    for k, out in enumerate((first_ref, second_ref)):
        at_end = even_sub if k == 0 else 1 - even_sub
        row = pl.ds(at_end * (height - 1), 1)
        for n in (0, 2):
            one, two = one_ref[n, row, :], two_ref[n, row, :]
            out[n, 0:1, :] = jnp.where(even_cell, two, one)
            out[n, last : last + 1, :] = jnp.where(even_cell, one, two)


def corners(cells, lines, after):
    vmem = pl.BlockSpec(memory_space=pltpu.VMEM)
    line = jax.ShapeDtypeStruct(lines[0].shape, jnp.float32)
    return pl.pallas_call(
        corners_kernel,
        out_shape=(line, line),
        in_specs=[vmem] * 4 + [pl.BlockSpec(memory_space=pl.ANY)],
        out_specs=(vmem, vmem),
        compiler_params=pltpu.CompilerParams(vmem_limit_bytes=8 * 2**20),
        name="corners",
    )(*cells, *lines, after)


def swap_pairs(first_sent, second_sent, axis):
    count = lax.axis_size(axis)
    first = [(i, i ^ 1) for i in range(count)]
    second = [(i, i + 1) for i in range(1, count - 1, 2)]
    second = second + [(j, i) for i, j in second]
    return lax.ppermute(first_sent, axis, first), lax.ppermute(second_sent, axis, second)


def load_code(face_dof, unknowns):
    patch, unknown = face_dof // unknowns, face_dof % unknowns
    return ((unknown // LANES * 8 + patch) * LANES + unknown % LANES).astype(jnp.float32)


def on_device(
    source,
    permeability,
    storage,
    face_cell,
    face_dest,
    face_dof,
    face_weight,
    tectonic_load,
    patch_matrix,
    yield_limit,
    free_mask,
    step_kind,
):
    planes, height, depth = source.shape
    sides = edges(source, permeability, storage)
    cells = swap_pairs(*sides, "cell")
    *inner, first, second = image_inside(source, permeability, storage)
    dest = face_dest[:, 0]
    sent, slots, picker, table = face_slots(
        source, face_cell & (LANES - 1), dest, load_code(face_dof, tectonic_load.shape[1]), face_weight
    )
    lines = corners(cells, (first, second), sent)
    subs = swap_pairs(*lines, "sub")
    where = (face_cell >> 7) % 2 * (planes * height) + (face_cell >> 8)
    sent = add_values(where, dest, slots, picker, sent, table)
    image, sent = norms(
        where, dest, (slots, picker, sent), sides, cells, lines, subs, inner, source, storage
    )
    got = lax.all_to_all(sent, AXES, 0, 0, tiled=True)
    pressure_change, slip = finish(
        got, tectonic_load, yield_limit, free_mask, step_kind, patch_matrix, source, image
    )
    return (pressure_change, slip)


def solution(mesh):
    return jax.shard_map(
        on_device,
        mesh=mesh,
        in_specs=(
            P("cell", "sub", None),
            P("cell", "sub", None),
            P("cell", "sub", None),
            P(("cell", "sub")),
            P(("cell", "sub"), None),
            P(("cell", "sub")),
            P(("cell", "sub")),
            P(("cell", "sub"), None),
            P(("cell", "sub"), None, None),
            P(("cell", "sub"), None),
            P(None, ("cell", "sub"), None),
            P(None, ("cell", "sub")),
        ),
        out_specs=(P("cell", "sub", None), P(("cell", "sub"), None)),
        check_vma=False,
    )
```

```python
import functools

import jax
import jax.numpy as jnp
from jax import lax
from jax.experimental import pallas as pl
from jax.experimental.pallas import tpu as pltpu
from jax.sharding import PartitionSpec as P

SLOTS = 32
AXES = ("cell", "sub")
LANES = 128
EDGES = 61 * 2**20
INSIDE = 46 * 2**20
UNROLL = 2


def split3(values):
    first = values.astype(jnp.bfloat16).astype(jnp.float32)
    left = values - first
    second = left.astype(jnp.bfloat16).astype(jnp.float32)
    return first, second, left - second


def onehot(values):
    return values.astype(jnp.float32).astype(jnp.bfloat16)


def dot(left, right):
    return jnp.dot(left, right, preferred_element_type=jnp.float32)


def pieces_of(values):
    return jnp.concatenate([piece.astype(jnp.bfloat16) for piece in split3(values)], axis=1)


def spread_columns(columns, chunks):
    shape = (columns.shape[1], chunks * LANES)
    take = lax.broadcasted_iota(jnp.int32, shape, 0) % chunks == lax.broadcasted_iota(jnp.int32, shape, 1) // LANES
    return dot(columns, onehot(take))


def sum_lanes(values):
    return dot(pieces_of(values), jnp.ones((3 * LANES, LANES), jnp.bfloat16))


def grouped_pieces(value, slots):
    lane = lax.broadcasted_iota(jnp.int32, value.shape, 1)
    first, second, third = split3(value)
    piece = jnp.where(lane < SLOTS, first, jnp.where(lane < 2 * SLOTS, second, third))
    return jnp.where(slots > 0.0, piece, 0.0).astype(jnp.bfloat16)


def join_groups(summed, group):
    lane = lax.broadcasted_iota(jnp.int32, summed.shape, 1)
    joined = summed + pltpu.roll(summed, LANES - SLOTS, 1) + pltpu.roll(summed, LANES - 2 * SLOTS, 1)
    if group:
        joined = pltpu.roll(joined, group * SLOTS, 1)
    return jnp.where((lane >= group * SLOTS) & (lane < (group + 1) * SLOTS), joined, 0.0)


def copy_rows(table, picks, where_ref, first, count):
    for j in range(count):
        picks[pl.ds(first + j, 1), :] = table[pl.ds(where_ref[first + j], 1), :]


def slots_kernel(
    dest_ref,
    code_ref,
    weight_ref,
    lane_ref,
    source_ref,
    sent_ref,
    slots_ref,
    picker_ref,
    table_ref,
    owners,
    spread,
    sems,
):
    chunks = dest_ref.shape[0]
    rows = source_ref.shape[0]
    halves = [
        pltpu.make_async_copy(
            source_ref.at[:, pl.ds(t * LANES, LANES)], table_ref.at[pl.ds(t * rows, rows), :], sems.at[t]
        )
        for t in range(2)
    ]
    for half in halves:
        half.start()
    dest = dest_ref[...].astype(jnp.float32)
    lane = lax.broadcasted_iota(jnp.int32, (LANES, LANES), 1)
    row = lax.broadcasted_iota(jnp.int32, (LANES, LANES), 0)
    lower = onehot(lane < row)
    lane_number = lane.astype(jnp.float32)
    row_number = row.astype(jnp.float32)
    ones = jnp.ones((LANES, LANES), jnp.bfloat16)
    dest_spread = spread_columns(dest.T.astype(jnp.bfloat16), chunks)
    lane_spread = spread_columns(lane_ref[...].astype(jnp.float32).T.astype(jnp.bfloat16), chunks)
    weight_spread = spread_columns(pieces_of(weight_ref[...].T), chunks)
    code_spread = spread_columns(pieces_of(code_ref[...].T), chunks)
    start = jnp.zeros((1, LANES), jnp.float32)
    for c in range(chunks):
        span = pl.ds(c * LANES, LANES)
        cut = slice(c * LANES, (c + 1) * LANES)
        named = (lane_number == dest_spread[:, cut]).astype(jnp.float32)
        ahead = dot(lower, named.astype(jnp.bfloat16))
        rank = dot((named * (ahead + start)).astype(jnp.bfloat16), ones)
        start = start + jnp.sum(named, axis=0, keepdims=True)
        here = ((lane & (SLOTS - 1)).astype(jnp.float32) == rank) & (lane < 3 * SLOTS)
        slots = here.astype(jnp.float32)
        slots_ref[:, span] = slots.astype(jnp.bfloat16)
        picker_ref[:, span] = jnp.where(lane_number == lane_spread[:, cut], weight_spread[:, cut], 0.0)
        owners[:, span] = onehot(row_number == dest[c : c + 1, :])
        spread[span, :] = grouped_pieces(code_spread[:, cut], slots)
    sent_ref[...] = join_groups(dot(owners[...], spread[...]), 0)
    for half in halves:
        half.wait()


def values_kernel(
    where_ref, dest_ref, slots_ref, picker_ref, sent_in_ref, table_ref, sent_ref, picks, owners, spread
):
    chunks = dest_ref.shape[0]

    def gather(i, carry):
        copy_rows(table_ref, picks, where_ref, i * 64, 64)
        return carry

    lax.fori_loop(0, chunks * LANES // 64, gather, 0)
    face_values(dest_ref, slots_ref, picker_ref, picks, owners, spread)
    sent_ref[...] = sent_in_ref[...] + join_groups(dot(owners[...], spread[...]), 1)


def face_values(dest_ref, slots_ref, picker_ref, picks, owners, spread):
    dest = dest_ref[...]
    owner = lax.broadcasted_iota(jnp.int32, (LANES, LANES), 0)
    for c in range(dest.shape[0]):
        span = pl.ds(c * LANES, LANES)
        owners[:, span] = onehot(owner == dest[c : c + 1, :])
        value = sum_lanes(picks[span, :] * picker_ref[:, span])
        spread[span, :] = grouped_pieces(value, slots_ref[:, span].astype(jnp.float32))


def face_slots(source, lane, dest, code, weight):
    count = dest.shape[0]
    chunks = count // LANES
    rows = source.shape[0] * source.shape[1]
    vmem = pl.BlockSpec(memory_space=pltpu.VMEM)
    cut = lambda values: values.reshape(chunks, LANES)
    return pl.pallas_call(
        slots_kernel,
        out_shape=(
            jax.ShapeDtypeStruct((LANES, LANES), jnp.float32),
            jax.ShapeDtypeStruct((LANES, count), jnp.bfloat16),
            jax.ShapeDtypeStruct((LANES, count), jnp.float32),
            jax.ShapeDtypeStruct((2 * rows, LANES), jnp.float32),
        ),
        in_specs=[vmem] * 4 + [pl.BlockSpec(memory_space=pl.ANY)],
        out_specs=(vmem,) * 4,
        scratch_shapes=[
            pltpu.VMEM((LANES, count), jnp.bfloat16),
            pltpu.VMEM((count, LANES), jnp.bfloat16),
            pltpu.SemaphoreType.DMA((2,)),
        ],
        compiler_params=pltpu.CompilerParams(vmem_limit_bytes=8 * 2**20),
        name="slots",
    )(cut(dest), cut(code), cut(weight), cut(lane), source.reshape(rows, source.shape[2]))


def add_values(where, dest, slots, picker, sent, table):
    count = where.shape[0]
    vmem = pl.BlockSpec(memory_space=pltpu.VMEM)
    return pl.pallas_call(
        values_kernel,
        out_shape=jax.ShapeDtypeStruct((LANES, LANES), jnp.float32),
        in_specs=[pl.BlockSpec(memory_space=pltpu.SMEM)] + [vmem] * 5,
        out_specs=vmem,
        scratch_shapes=[
            pltpu.VMEM((count, LANES), jnp.float32),
            pltpu.VMEM((LANES, count), jnp.bfloat16),
            pltpu.VMEM((count, LANES), jnp.bfloat16),
        ],
        compiler_params=pltpu.CompilerParams(vmem_limit_bytes=8 * 2**20),
        name="values",
    )(where, dest.reshape(count // LANES, LANES), slots, picker, sent, table)


def image_kernel(
    source_ref,
    perm_ref,
    storage_ref,
    image_ref,
    con_x_ref,
    con_y_ref,
    con_z_ref,
    sums_ref,
    first_ref,
    second_ref,
    field,
    half,
    store,
    carry_x,
    sems,
):
    planes, height, depth = source_ref.shape
    strips = height // 8
    group = 8
    copies = []
    for g in range(planes // group):
        span = pl.ds(g * group, group)
        for n, (array, held) in enumerate(((source_ref, field), (perm_ref, half), (storage_ref, store))):
            copies.append(pltpu.make_async_copy(array.at[span], held.at[span], sems.at[3 * g + n]))
    for copy in copies:
        copy.start()
    lane = lax.broadcasted_iota(jnp.int32, (8, depth), 1)
    row = lax.broadcasted_iota(jnp.int32, (8, depth), 0)
    zero = jnp.zeros((8, depth), jnp.float32)

    even = is_even("sub")
    for out in (first_ref, second_ref):
        for n in range(len(WANTED)):
            out[n, 0:8, :] = zero
            out[n, planes : planes + 8, :] = zero

    def send_rows(x):
        for k, out in enumerate((first_ref, second_ref)):
            at_end = even if k == 0 else 1 - even
            for n, (f, deep) in enumerate(WANTED):
                row = deep + at_end * (height - 1 - 2 * deep)
                out[n, pl.ds(x + 1, 1), :] = (field, half, store)[f][x, pl.ds(row, 1), :]

    def plane(x, sums, last):
        if not last:
            send_rows(x + 1)
            half[x + 1] = half_of(half[x + 1])
        square, product = sums
        last_y = zero
        for i in range(strips):
            at = 8 * i
            rows = pl.ds(at, 8)
            b, h = field[x, rows, :], half[x, rows, :]
            if i + 1 < strips:
                b_y, h_y = field[x, pl.ds(at + 1, 8), :], half[x, pl.ds(at + 1, 8), :]
                c_y = 1.0 / (h + h_y)
            else:
                b_y, h_y = pltpu.roll(b, 7, 0), pltpu.roll(h, 7, 0)
                c_y = jnp.where(row == 7, 0.0, 1.0 / (h + h_y))
            c_z = jnp.where(lane == depth - 1, 0.0, 1.0 / (h + pltpu.roll(h, depth - 1, 1)))
            f_y, f_z = c_y * (b - b_y), c_z * (b - pltpu.roll(b, depth - 1, 1))
            came_y = pltpu.roll(jnp.where(row == 7, last_y, f_y), 1, 0)
            last_y = f_y
            w = store[x, rows, :] * b + (f_y - came_y) + (f_z - pltpu.roll(f_z, 1, 1)) - carry_x[rows, :]
            if last:
                c_x = zero
            else:
                c_x = 1.0 / (h + half[x + 1, rows, :])
                f_x = c_x * (b - field[x + 1, rows, :])
                carry_x[rows, :] = f_x
                w = w + f_x
            image_ref[x, rows, :] = w
            con_x_ref[x, rows, :] = c_x
            con_y_ref[x, rows, :] = c_y
            con_z_ref[x, rows, :] = c_z
            square = square + b * b
            product = product + b * w
        return square, product

    sums = (zero, zero)
    chunks = planes // group
    for copy in copies[:3]:
        copy.wait()
    send_rows(0)
    half[0] = half_of(half[0])
    carry_x[...] = jnp.zeros_like(carry_x)
    for g in range(chunks):
        for copy in copies[3 * g + 3 : 3 * g + 6]:
            copy.wait()
        runs = group // UNROLL if g + 1 < chunks else group // UNROLL - 1

        def run(n, sums):
            for u in range(UNROLL):
                sums = plane(g * group + n * UNROLL + u, sums, False)
            return sums

        sums = lax.fori_loop(0, runs, run, sums)
    for x in range(planes - UNROLL, planes - 1):
        sums = plane(x, sums, False)
    square, product = plane(planes - 1, sums, True)
    sums_ref[0] = square
    sums_ref[1] = product


def half_of(perm):
    return 0.5 / jnp.maximum(perm, 1e-30)


def image_inside(source, permeability, storage):
    planes, height, depth = source.shape
    vmem = pl.BlockSpec(memory_space=pltpu.VMEM)
    block = jax.ShapeDtypeStruct(source.shape, jnp.float32)
    held = pltpu.VMEM(source.shape, jnp.float32)
    line = jax.ShapeDtypeStruct((5, planes + 8, depth), jnp.float32)
    return pl.pallas_call(
        image_kernel,
        out_shape=(block,) * 4 + (jax.ShapeDtypeStruct((2, 8, depth), jnp.float32), line, line),
        in_specs=[pl.BlockSpec(memory_space=pl.ANY)] * 3,
        out_specs=(vmem,) * 7,
        scratch_shapes=[
            held,
            held,
            held,
            pltpu.VMEM((height, depth), jnp.float32),
            pltpu.SemaphoreType.DMA((3 * planes // 8,)),
        ],
        compiler_params=pltpu.CompilerParams(vmem_limit_bytes=INSIDE),
        name="image",
    )(source, permeability, storage)


def norms_kernel(
    where_ref,
    dest_ref,
    slots_ref,
    picker_ref,
    sent_in_ref,
    side_first_ref,
    side_second_ref,
    cell_first_ref,
    cell_second_ref,
    line_first_ref,
    line_second_ref,
    sub_first_ref,
    sub_second_ref,
    part_ref,
    con_x_ref,
    con_y_ref,
    con_z_ref,
    sums_ref,
    source_ref,
    storage_ref,
    image_ref,
    sent_ref,
    rest,
    flows,
    lines,
    table,
    picks,
    owners,
    spread,
):
    planes, height, depth = source_ref.shape
    strips = height // 8
    even_cell = is_even("cell") == 1
    even_sub = is_even("sub") == 1

    def total(values):
        return jnp.sum(jnp.sum(values, axis=1, keepdims=True), axis=0, keepdims=True)

    def conduct(one, other):
        return 1.0 / (half_of(one) + half_of(other))

    def along_depth(b, k):
        lane = lax.broadcasted_iota(jnp.int32, b.shape, 1)
        flow = conduct(k, pltpu.roll(k, depth - 1, 1)) * (b - pltpu.roll(b, depth - 1, 1))
        flow = jnp.where(lane == depth - 1, 0.0, flow)
        return flow - pltpu.roll(flow, 1, 1)

    def cell_side(n):
        one, two = cell_first_ref[n], cell_second_ref[n]
        return jnp.where(even_cell, two, one), jnp.where(even_cell, one, two)

    def own_side(n):
        one, two = side_first_ref[n], side_second_ref[n]
        return jnp.where(even_cell, two, one), jnp.where(even_cell, one, two)

    b_lo, b_hi = cell_side(0)
    b_far = cell_side(1)[1]
    k_lo, k_hi = cell_side(2)
    k_far = cell_side(3)[1]
    s_hi = cell_side(4)[1]
    b_head, b_tail = own_side(0)
    k_head, k_tail = own_side(2)
    con_hi = conduct(k_tail, k_hi)
    flow_lo = conduct(k_lo, k_head) * (b_lo - b_head)
    flow_hi = con_hi * (b_tail - b_hi)

    def sub_side(n):
        one, two = sub_first_ref[n], sub_second_ref[n]
        return jnp.where(even_sub, two, one), jnp.where(even_sub, one, two)

    def own_line(n):
        one, two = line_first_ref[n], line_second_ref[n]
        return jnp.where(even_sub, two, one), jnp.where(even_sub, one, two)

    by_lo, by_hi = sub_side(0)
    by_far = sub_side(1)[1]
    ky_lo, ky_hi = sub_side(2)
    ky_far = sub_side(3)[1]
    sy_hi = sub_side(4)[1]
    by_head, by_tail = own_line(0)
    ky_head, ky_tail = own_line(2)
    cony_hi = conduct(ky_tail, ky_hi)
    flowy_lo = conduct(ky_lo, ky_head) * (by_lo - by_head)
    flowy_hi = cony_hi * (by_tail - by_hi)
    count = by_lo.shape[0]
    number = lax.broadcasted_iota(jnp.int32, by_lo.shape, 0)
    inside = (number >= 1) & (number <= planes)

    row = lax.broadcasted_iota(jnp.int32, b_hi.shape, 0)
    flow = conduct(k_hi, pltpu.roll(k_hi, height - 1, 0)) * (b_hi - pltpu.roll(b_hi, height - 1, 0))
    flow = jnp.where(row == height - 1, flowy_hi[planes + 1 : planes + 2], flow)
    came = jnp.where(row == 0, flowy_lo[planes + 1 : planes + 2], pltpu.roll(flow, 1, 0))
    w_hi = s_hi * b_hi + (conduct(k_hi, k_far) * (b_hi - b_far) - flow_hi) + (flow - came)
    w_hi = w_hi + along_depth(b_hi, k_hi)

    flow = conduct(ky_hi, pltpu.roll(ky_hi, count - 1, 0)) * (by_hi - pltpu.roll(by_hi, count - 1, 0))
    wy_hi = sy_hi * by_hi + (conduct(ky_hi, ky_far) * (by_hi - by_far) - flowy_hi)
    wy_hi = wy_hi + (flow - pltpu.roll(flow, 1, 0)) + along_depth(by_hi, ky_hi)

    def rows_total(values):
        return total(jnp.where(inside, values, 0.0))

    square = total(sums_ref[0])
    lower = total(flow_lo * b_head) + rows_total(flowy_lo * by_head)
    product = total(sums_ref[1]) - lower + total(flow_hi * b_tail) + rows_total(flowy_hi * by_tail)
    bb = product - total(flow_hi * b_hi) - rows_total(flowy_hi * by_hi) + lower
    some = square > 0.0
    mu = jnp.where(some, product / jnp.where(some, square, 1.0), 0.0)

    flows[0] = flowy_lo
    flows[1] = flowy_hi
    lines[...] = jnp.zeros_like(lines)
    strip_row = lax.broadcasted_iota(jnp.int32, (8, depth), 0)

    def complete(x, extra):
        for i in range(strips):
            rows = pl.ds(8 * i, 8)
            w = part_ref[x, rows, :]
            if extra is not None:
                w = w + extra[8 * i : 8 * i + 8]
            if i == 0:
                w = w - jnp.where(strip_row == 0, flows[0, pl.ds(x + 1, 1), :], 0.0)
            if i == strips - 1:
                w = w + jnp.where(strip_row == 7, flows[1, pl.ds(x + 1, 1), :], 0.0)
            image_ref[x, rows, :] = w
            for t in range(2):
                table[pl.ds(pl.multiple_of((t * planes + x) * height, 8) + 8 * i, 8), :] = w[
                    :, t * LANES : (t + 1) * LANES
                ]
            v = w - mu * source_ref[x, rows, :]
            rest[x, rows, :] = v
            if i == 0:
                lines[0, pl.ds(x + 1, 1), :] = v[0:1]
            if i == strips - 1:
                lines[1, pl.ds(x + 1, 1), :] = v[7:8]

    complete(0, -flow_lo)

    def middle(x, carry):
        complete(x, None)
        return carry

    lax.fori_loop(0, planes // 2 - 1, lambda n, c: middle(2 * n + 2, middle(2 * n + 1, c)), 0)
    complete(planes - 1, flow_hi)
    v_hi = w_hi - mu * b_hi
    vy_hi = wy_hi - mu * by_hi
    rest[planes] = v_hi

    each = where_ref.shape[0] // planes

    def measure(x, sums):
        vv, vav = sums
        copy_rows(table, picks, where_ref, x * each, each)
        for i in range(strips):
            rows = pl.ds(8 * i, 8)
            v = rest[x, rows, :]
            d_x = v - rest[x + 1, rows, :]
            if i + 1 < strips:
                d_y = v - rest[x, pl.ds(8 * i + 1, 8), :]
            else:
                d_y = v - pltpu.roll(v, 7, 0)
            d_z = v - pltpu.roll(v, depth - 1, 1)
            squared = v * v
            vv = vv + squared
            vav = vav + (storage_ref[x, rows, :] * squared + con_x_ref[x, rows, :] * (d_x * d_x)) + (
                con_y_ref[x, rows, :] * (d_y * d_y) + con_z_ref[x, rows, :] * (d_z * d_z)
            )
        return vv, vav

    zero = jnp.zeros((8, depth), jnp.float32)
    sums = lax.fori_loop(0, planes // 2, lambda n, s: measure(2 * n + 1, measure(2 * n, s)), (zero, zero))
    vv, vav = [total(values) for values in sums]
    v_head, v_tail = rest[0], rest[planes - 1]
    vy_head, vy_tail = lines[0], lines[1]
    bv = vv - total(flow_hi * v_hi) - rows_total(flowy_hi * vy_hi)
    bv = bv + total(flow_lo * v_head) + rows_total(flowy_lo * vy_head)
    vav = vav + total(con_hi * ((v_tail - v_hi) * (v_tail - v_hi)))
    vav = vav + rows_total(cony_hi * ((vy_tail - vy_hi) * (vy_tail - vy_hi)))

    face_values(dest_ref, slots_ref, picker_ref, picks, owners, spread)
    summed = dot(owners[...], spread[...])
    sent = sent_in_ref[...] + join_groups(summed, 2)
    place = lax.broadcasted_iota(jnp.int32, sent.shape, 1)
    for n, scalar in enumerate((square, mu, vv, bb, bv, vav)):
        sent = jnp.where(place == 3 * SLOTS + n, scalar, sent)
    sent_ref[...] = sent


def norms(where, dest, marks, sides, cells, lines, subs, inner, source, storage):
    planes, height, depth = source.shape
    count = where.shape[0]
    chunks = count // LANES
    vmem = pl.BlockSpec(memory_space=pltpu.VMEM)
    smem = pl.BlockSpec(memory_space=pltpu.SMEM)
    line = pltpu.VMEM((2,) + lines[0].shape[1:], jnp.float32)
    operands = (dest.reshape(chunks, LANES), *marks, *sides, *cells, *lines, *subs, *inner, source, storage)
    return pl.pallas_call(
        norms_kernel,
        out_shape=(
            jax.ShapeDtypeStruct(source.shape, jnp.float32),
            jax.ShapeDtypeStruct((LANES, LANES), jnp.float32),
        ),
        in_specs=[smem] + [vmem] * len(operands),
        out_specs=(vmem, vmem),
        scratch_shapes=[
            pltpu.VMEM((planes + 1, height, depth), jnp.float32),
            line,
            line,
            pltpu.VMEM((2 * planes * height, LANES), jnp.float32),
            pltpu.VMEM((count, LANES), jnp.float32),
            pltpu.VMEM((LANES, count), jnp.bfloat16),
            pltpu.VMEM((count, LANES), jnp.bfloat16),
        ],
        compiler_params=pltpu.CompilerParams(vmem_limit_bytes=12 * 2**20),
        name="norms",
    )(where, *operands)


def final_kernel(
    steps,
    kind_ref,
    got_ref,
    tectonic_ref,
    yield_ref,
    free_ref,
    matrix_ref,
    source_ref,
    image_ref,
    pressure_ref,
    slip_ref,
    pressure,
    wide,
    tall,
    turned,
    sem,
):
    patches, unknowns = tectonic_ref.shape
    tiles = unknowns // LANES
    got = got_ref[...]
    across = got.T
    scal = [across[3 * SLOTS + i : 3 * SLOTS + i + 1, :] for i in range(6)]
    square, mu, rest_sq, bb, bv, vv = scal

    def total(row):
        return jnp.sum(row, axis=1, keepdims=True)

    norm = total(square)
    alpha = norm / total(bb)
    part = 1.0 - alpha * mu
    edge = part * jnp.sqrt(square)
    norm_next = total(edge * edge + alpha * alpha * rest_sq)
    beta = norm_next / norm
    part = part + beta
    curve = total(part * part * bb - 2.0 * part * alpha * bv + alpha * alpha * vv)
    alpha_next = norm_next / curve
    on_source = alpha + alpha_next * (1.0 + beta)
    on_image = -alpha_next * alpha

    count = got.shape[0]
    code = got[:, :SLOTS].astype(jnp.int32)
    code_across = across[:SLOTS].astype(jnp.int32)
    terms = on_source * across[SLOTS : 2 * SLOTS] + on_image * across[2 * SLOTS : 3 * SLOTS]
    pieces = split3(terms)
    lane = lax.broadcasted_iota(jnp.int32, (count, LANES), 1)
    high = lax.broadcasted_iota(jnp.int32, (8 * tiles, count), 0)
    low_code = code & (LANES - 1)
    high_code = code_across >> 7
    for slot in range(SLOTS):
        span = pl.ds(slot * count, count)
        wide[span, :] = (lane == low_code[:, slot : slot + 1]).astype(jnp.float32).astype(jnp.bfloat16)
        here = high == high_code[slot : slot + 1, :]
        for index, piece in enumerate(pieces):
            tall[pl.ds(index * 8 * tiles, 8 * tiles), span] = jnp.where(
                here, piece[slot : slot + 1, :], 0.0
            ).astype(jnp.bfloat16)
    summed = jnp.dot(tall[...], wide[...], preferred_element_type=jnp.float32)
    summed = summed[: 8 * tiles] + summed[8 * tiles : 16 * tiles] + summed[16 * tiles :]
    loads = jnp.concatenate([summed[8 * t : 8 * t + 8] for t in range(tiles)], axis=1)
    fault_load = tectonic_ref[...] + loads[:patches]

    for x in range(0, source_ref.shape[0], 4):
        pressure[x : x + 4] = on_source[None] * source_ref[x : x + 4] + on_image[None] * image_ref[x : x + 4]

    leaving = pltpu.make_async_copy(pressure, pressure_ref, sem)
    leaving.start()

    piece_row = lax.broadcasted_iota(jnp.int32, (16, patches * LANES), 0)
    piece_lane = lax.broadcasted_iota(jnp.int32, (16, patches * LANES), 1)
    choose = onehot((piece_row & 3) == (piece_lane >> 7))

    place = lax.broadcasted_iota(jnp.int32, (8, unknowns), 0)

    def fold(one, other, step):
        return jnp.where(
            place & step == 0, one + pltpu.roll(one, 8 - step, 0), other + pltpu.roll(other, step, 0)
        )

    def times_matrix(vector):
        pieces = jnp.concatenate([*split3(vector), jnp.zeros_like(vector)], axis=0)
        turned[...] = lax.dot_general(
            pieces.astype(jnp.bfloat16), choose, (((0,), (0,)), ((), ())), preferred_element_type=jnp.float32
        )
        group = 16

        def body(i, sums):
            sums = list(sums)
            for g in range(group):
                start = pl.multiple_of(i * (8 * group), 8 * group) + 8 * g
                for p in range(patches):
                    spread = turned[pl.ds(start, 8), p * LANES : (p + 1) * LANES]
                    sums[p] = sums[p] + matrix_ref[p, pl.ds(start, 8), :] * jnp.concatenate(
                        [spread] * tiles, axis=1
                    )
            return tuple(sums)

        zero = jnp.zeros((8, unknowns), jnp.float32)
        sums = lax.fori_loop(0, unknowns // (8 * group), body, (zero,) * patches)
        low, high = fold(sums[0], sums[1], 1), fold(sums[2], sums[3], 1)
        both = fold(low, high, 2)
        return (both + pltpu.roll(both, 4, 0))[:patches]

    def mean(values):
        return jnp.sum(values, axis=1, keepdims=True) * (1.0 / unknowns)

    limit = yield_ref[...]
    row = lax.broadcasted_iota(jnp.int32, (patches, unknowns), 0)
    slip_now = None
    previous = None
    previous_image = None
    for iteration in range(steps):
        if iteration == 0:
            gradient = -fault_load
        else:
            gradient = times_matrix(slip_now) - fault_load
        free_part = jnp.where(free_ref[iteration] == 1, gradient, 0.0)
        kind = jnp.zeros((patches, unknowns), jnp.int32)
        for p in range(patches):
            kind = jnp.where(row == p, kind_ref[iteration, p], kind)
        conjugate = free_part
        if iteration > 0:
            conjugacy = mean(free_part * previous_image) / curved
            conjugate = free_part - conjugacy * previous
        direction = jnp.where(
            kind == 0, conjugate, jnp.where(kind == 1, gradient - free_part, gradient)
        )
        image_vec = times_matrix(direction)
        curved = mean(direction * image_vec) + 1e-06
        step_length = mean(gradient * direction) / curved
        moved = -step_length * direction if iteration == 0 else slip_now - step_length * direction
        slip_now = jnp.clip(moved, -limit, limit)
        previous = direction
        previous_image = image_vec
    slip_ref[...] = slip_now
    leaving.wait()


def finish(got, tectonic_load, yield_limit, free_mask, step_kind, patch_matrix, source, image):
    patches, unknowns = tectonic_load.shape
    tiles = unknowns // LANES
    count = got.shape[0]
    vmem = pl.BlockSpec(memory_space=pltpu.VMEM)
    return pl.pallas_call(
        functools.partial(final_kernel, step_kind.shape[0]),
        out_shape=(
            jax.ShapeDtypeStruct(source.shape, jnp.float32),
            jax.ShapeDtypeStruct(tectonic_load.shape, jnp.float32),
        ),
        in_specs=[pl.BlockSpec(memory_space=pltpu.SMEM)] + [vmem] * 7,
        out_specs=(pl.BlockSpec(memory_space=pl.ANY), vmem),
        scratch_shapes=[
            pltpu.VMEM(source.shape, jnp.float32),
            pltpu.VMEM((SLOTS * count, LANES), jnp.bfloat16),
            pltpu.VMEM((24 * tiles, SLOTS * count), jnp.bfloat16),
            pltpu.VMEM((unknowns, patches * LANES), jnp.float32),
            pltpu.SemaphoreType.DMA,
        ],
        compiler_params=pltpu.CompilerParams(vmem_limit_bytes=20 * 2**20),
        name="finish",
    )(step_kind, got, tectonic_load, yield_limit, free_mask, patch_matrix, source, image)


def is_even(axis):
    return (lax.axis_index(axis) + 1) % 2


WANTED = ((0, 0), (0, 1), (1, 0), (1, 1), (2, 0))


def edges_kernel(source_ref, perm_ref, storage_ref, first_ref, second_ref, held, sems):
    planes = source_ref.shape[0]
    fields = (source_ref, perm_ref, storage_ref)
    even = is_even("cell")
    copies = []
    for n, (f, deep) in enumerate(WANTED):
        for k, out in enumerate((first_ref, second_ref)):
            at_end = even if k == 0 else 1 - even
            plane = deep + at_end * (planes - 1 - 2 * deep)
            at = 2 * n + k
            copies.append(
                (
                    pltpu.make_async_copy(fields[f].at[plane], held.at[at], sems.at[at]),
                    pltpu.make_async_copy(held.at[at], out.at[n], sems.at[10 + at]),
                )
            )
    for arriving, _ in copies:
        arriving.start()
    for arriving, leaving in copies:
        arriving.wait()
        leaving.start()
    for _, leaving in copies:
        leaving.wait()


def edges(source, permeability, storage):
    side = jax.ShapeDtypeStruct((5,) + source.shape[1:], jnp.float32)
    return pl.pallas_call(
        edges_kernel,
        out_shape=(side, side),
        in_specs=[pl.BlockSpec(memory_space=pl.ANY)] * 3,
        out_specs=(pl.BlockSpec(memory_space=pl.ANY),) * 2,
        scratch_shapes=[
            pltpu.VMEM((10,) + source.shape[1:], jnp.float32),
            pltpu.SemaphoreType.DMA((20,)),
        ],
        compiler_params=pltpu.CompilerParams(vmem_limit_bytes=EDGES),
        name="edges",
    )(source, permeability, storage)


def corners_kernel(one_ref, two_ref, first_in_ref, second_in_ref, after_ref, first_ref, second_ref):
    height = one_ref.shape[1]
    last = first_ref.shape[1] - 7
    even_cell = is_even("cell") == 1
    even_sub = is_even("sub")
    first_ref[...] = first_in_ref[...]
    second_ref[...] = second_in_ref[...]
    for k, out in enumerate((first_ref, second_ref)):
        at_end = even_sub if k == 0 else 1 - even_sub
        row = pl.ds(at_end * (height - 1), 1)
        for n in (0, 2):
            one, two = one_ref[n, row, :], two_ref[n, row, :]
            out[n, 0:1, :] = jnp.where(even_cell, two, one)
            out[n, last : last + 1, :] = jnp.where(even_cell, one, two)


def corners(cells, lines, after):
    vmem = pl.BlockSpec(memory_space=pltpu.VMEM)
    line = jax.ShapeDtypeStruct(lines[0].shape, jnp.float32)
    return pl.pallas_call(
        corners_kernel,
        out_shape=(line, line),
        in_specs=[vmem] * 4 + [pl.BlockSpec(memory_space=pl.ANY)],
        out_specs=(vmem, vmem),
        compiler_params=pltpu.CompilerParams(vmem_limit_bytes=8 * 2**20),
        name="corners",
    )(*cells, *lines, after)


def swap_pairs(first_sent, second_sent, axis):
    count = lax.axis_size(axis)
    first = [(i, i ^ 1) for i in range(count)]
    second = [(i, i + 1) for i in range(1, count - 1, 2)]
    second = second + [(j, i) for i, j in second]
    return lax.ppermute(first_sent, axis, first), lax.ppermute(second_sent, axis, second)


def load_code(face_dof, unknowns):
    patch, unknown = face_dof // unknowns, face_dof % unknowns
    return ((unknown // LANES * 8 + patch) * LANES + unknown % LANES).astype(jnp.float32)


def on_device(
    source,
    permeability,
    storage,
    face_cell,
    face_dest,
    face_dof,
    face_weight,
    tectonic_load,
    patch_matrix,
    yield_limit,
    free_mask,
    step_kind,
):
    planes, height, depth = source.shape
    sides = edges(source, permeability, storage)
    cells = swap_pairs(*sides, "cell")
    *inner, first, second = image_inside(source, permeability, storage)
    dest = face_dest[:, 0]
    sent, slots, picker, table = face_slots(
        source, face_cell & (LANES - 1), dest, load_code(face_dof, tectonic_load.shape[1]), face_weight
    )
    lines = corners(cells, (first, second), sent)
    subs = swap_pairs(*lines, "sub")
    where = (face_cell >> 7) % 2 * (planes * height) + (face_cell >> 8)
    sent = add_values(where, dest, slots, picker, sent, table)
    image, sent = norms(
        where, dest, (slots, picker, sent), sides, cells, lines, subs, inner, source, storage
    )
    got = lax.all_to_all(sent, AXES, 0, 0, tiled=True)
    pressure_change, slip = finish(
        got, tectonic_load, yield_limit, free_mask, step_kind, patch_matrix, source, image
    )
    return (pressure_change, slip)


def solution(mesh):
    return jax.shard_map(
        on_device,
        mesh=mesh,
        in_specs=(
            P("cell", "sub", None),
            P("cell", "sub", None),
            P("cell", "sub", None),
            P(("cell", "sub")),
            P(("cell", "sub"), None),
            P(("cell", "sub")),
            P(("cell", "sub")),
            P(("cell", "sub"), None),
            P(("cell", "sub"), None, None),
            P(("cell", "sub"), None),
            P(None, ("cell", "sub"), None),
            P(None, ("cell", "sub")),
        ),
        out_specs=(P("cell", "sub", None), P(("cell", "sub"), None)),
        check_vma=False,
    )
```
